32 devices in a mesh: ctx: 16 (over z, y, x), pipe: 2 (over core).
Axes of the slice: x: 2, y: 2, z: 4, core: 2. Of those that a mesh axis runs over, the one named last changes fastest.
Arguments:
- loaded: bfloat16 [2, 32, 128, 4096], P('pipe', 'ctx'), may hold values from -6 to 6
- counts: int32 [16], P('ctx'), may hold values from 0 to 2, as said below
- destinations: int32 [32], P('ctx'), may hold values from -1 to 15, as said below
- bounds: int32 [16], replicated, may hold values from 0 to 128, as said below
- se_gate: bfloat16 [2, 2048, 4096], P('pipe', 'ctx'), may hold values from -6 to 6
- mr_gate: bfloat16 [2, 2048, 4096], P('pipe', 'ctx'), may hold values from -6 to 6
- phase_grads: bfloat16 [2, 2048, 4096], P('pipe', 'ctx'), may hold values from -6 to 6
- se_taps: float32 [2, 256, 7], P('pipe'), may hold values from -2.5 to 2.5
- mr_taps: float32 [2, 256, 128], P('pipe'), may hold values from -0.5 to 0.5
Outputs:
- grad_input: bfloat16 [2, 2048, 4096], P('pipe', 'ctx')
- grad_se_gate: bfloat16 [2, 2048, 4096], P('pipe', 'ctx')
- grad_mr_gate: bfloat16 [2, 2048, 4096], P('pipe', 'ctx')
- grad_se_taps: float32 [2, 256, 7], P('pipe')
- grad_mr_taps: float32 [2, 256, 128], P('pipe')
The draws below stay inside these ranges and needn't reach their ends.
Inputs may be any that keep to these rules, and one draw needn't show every extreme that they name: `counts`: loaders hold 0 to 2 tiles, 16 in all; taken loader by loader and slot by slot they are the sequence's tiles in order, and loader i's first tile is tile i or i + 1. The first loader holds 2 and the last holds none. `destinations`: entry 2 i + j is the sequence tile held in slot j of loader i, and -1 where j is not below that loader's count. `bounds`: entry t is the offset within tile t at which a new segment starts, at most one a tile, or 128 where none starts; tile 0's is 0 and the last tile's is 128.
All inputs are finite; a program needn't handle non-finite values.
Results may differ from the reference program's by a relative error of at most 0.0085.
Values may be sent and summed in bfloat16 or wider, within the bound.
No kernel may reach another device: no remote copies, remote signals or barrier semaphores. Data moves between devices by JAX's collectives and lax.ppermute only.
A program may use at most 192 MiB of HBM per device.

```python
import math
import jax
import jax.numpy as jnp
from jax import lax

CHANNELS = 4096
TILE = 128
SE_TAPS = 7
MR_TAPS = 128
GROUP = 16
TILES = 16
SLOTS = 32
TOKENS = 2048
GROUPS = 256


def route_plan(key):
    drift_bits = jax.random.randint(jax.random.fold_in(key, 11), (TILES + 1,), 0, 2)
    positions = jnp.arange(TILES + 1)
    drift_bits = jnp.where(positions == 0, 0, jnp.where(positions == TILES, 0, jnp.where(positions == 1, 1, jnp.where(positions == TILES - 1, 1, drift_bits))))
    held = 1 + drift_bits[1:] - drift_bits[:-1]
    return (drift_bits, held)


def draw_counts(key, part):
    drift_bits, held = route_plan(key)
    return held.astype(jnp.int32)


def draw_destinations(key, part):
    drift_bits, held = route_plan(key)
    loader = jnp.arange(TILES)
    first_tile = loader + drift_bits[:-1]
    paired = jnp.stack([first_tile, first_tile + 1], axis=1)
    living = jnp.arange(2)[None, :] < held[:, None]
    return jnp.where(living, paired, -1).reshape(-1).astype(jnp.int32)


def draw_bounds(key, part):
    cut_key = jax.random.fold_in(key, 23)
    none_key = jax.random.fold_in(key, 29)
    cut_at = jax.random.randint(cut_key, (TILES,), 0, TILE)
    without = jax.random.randint(none_key, (TILES,), 0, 2)
    offsets = jnp.where(without == 1, TILE, cut_at)
    positions = jnp.arange(TILES)
    offsets = jnp.where(positions == 0, 0, jnp.where(positions == TILES - 1, TILE, offsets))
    return offsets.astype(jnp.int32)


def level_of(rng, extent, split, smallest, largest):
    def one(position, shards_of):
        draws = jax.random.uniform(jax.random.fold_in(jax.random.fold_in(rng, 6), position), (shards_of,), jnp.float32, smallest / len(split), largest / len(split))
        return jnp.repeat(jnp.exp(draws), extent[position] // shards_of).reshape((-1,) + (1,) * (len(extent) - position - 1))

    loudness = one(*split[0])
    for cut in split[1:]:
        loudness = loudness * one(*cut)
    return loudness


def normal_values(rng, shape, deviation, bound, split=(), held_as=jnp.bfloat16):
    drawn = jax.random.normal(rng, shape, jnp.float32) * deviation
    if len(split) > 0:
        drawn = level_of(rng, shape, split, -0.22, 0.18) * drawn
    return jnp.clip(drawn, min=-bound, max=bound).astype(held_as)


def setup_inputs(seed: int = 0) -> dict:
    seeds = jax.random.split(jax.random.key(seed), 10)
    return {
        "loaded": normal_values(seeds[0], (2, SLOTS, TILE, CHANNELS), 1.0, 6.0, ((0, 2), (1, 16))),
        "counts": draw_counts(jax.random.fold_in(seeds[9], 71), 0),
        "destinations": draw_destinations(jax.random.fold_in(seeds[9], 71), 0),
        "bounds": draw_bounds(jax.random.fold_in(seeds[9], 71), 0),
        "se_gate": normal_values(seeds[4], (2, TOKENS, CHANNELS), 1.0, 6.0, ((0, 2), (1, 16))),
        "mr_gate": normal_values(seeds[5], (2, TOKENS, CHANNELS), 1.0, 6.0, ((0, 2), (1, 16))),
        "phase_grads": normal_values(seeds[6], (2, TOKENS, CHANNELS), 1.0, 6.0, ((0, 2), (1, 16))),
        "se_taps": normal_values(seeds[7], (2, GROUPS, SE_TAPS), 0.4, 2.5, ((0, 2),), jnp.float32),
        "mr_taps": normal_values(seeds[8], (2, GROUPS, MR_TAPS), 0.09, 0.5, ((0, 2),), jnp.float32),
    }


def toeplitz_rows(tap_table, starts):
    group_count = tap_table.shape[0]
    tap_count = tap_table.shape[1]
    row_count = starts.shape[0]
    col_count = 2 * tap_count
    tap_line = jnp.concatenate([jnp.zeros((group_count, 1), tap_table.dtype), tap_table[:, ::-1], jnp.zeros((group_count, col_count - tap_count), tap_table.dtype)], axis=1)
    spread_rows = jnp.broadcast_to(tap_line[:, None, :], (group_count, row_count, col_count + 1)).reshape(group_count, row_count * (col_count + 1))
    toeplitz = spread_rows[:, :row_count * col_count].reshape(group_count, row_count, col_count)
    columns = jnp.arange(col_count, dtype=jnp.int32)
    keep_mask = columns[None, :] - tap_count >= starts[:, None]
    return (jnp.where(keep_mask[None], toeplitz, jnp.zeros((), tap_table.dtype)), keep_mask)

def tap_sums(products):
    group_count = products.shape[0]
    row_count = products.shape[1]
    col_count = products.shape[2]
    flat = products.reshape(group_count, row_count * col_count)
    flat = jnp.pad(flat, ((0, 0), (0, row_count)))
    lagged = flat.reshape(group_count, row_count, col_count + 1)
    return lax.optimization_barrier(jnp.sum(lagged[:, :, 1:row_count + 1], axis=1))[:, ::-1]

def lag_grads(weighted, extended, keep_mask):
    pieces = 4
    row_count = weighted.shape[0]
    left_part = weighted.reshape(row_count, pieces, -1).transpose(1, 0, 2)
    right_part = extended.reshape(extended.shape[0], pieces, -1).transpose(1, 0, 2)

    def block_taps(operand_pair):
        front_part, back_part = operand_pair
        block_groups = front_part.shape[1] // GROUP
        products = jnp.einsum('rgc,sgc->grs', front_part.reshape(row_count, block_groups, GROUP), back_part.reshape(back_part.shape[0], block_groups, GROUP), preferred_element_type=jnp.float32)
        products = jnp.where(keep_mask[None], products, 0.0)
        return tap_sums(products)
    return lax.map(block_taps, (left_part, right_part)).reshape(-1, row_count)

def short_forward(extended, tap_table, starts):
    row_count = starts.shape[0]
    lead_rows = extended.shape[0] - row_count
    channel_taps = jnp.repeat(tap_table, GROUP, axis=0)
    positions = jnp.arange(row_count, dtype=jnp.int32)
    running = jnp.zeros((row_count, extended.shape[1]), jnp.float32)
    for offset in range(tap_table.shape[1]):
        shifted = extended[lead_rows - offset:lead_rows - offset + row_count].astype(jnp.float32)
        allowed = (positions - offset >= starts)[:, None]
        running = running + jnp.where(allowed, channel_taps[:, offset][None, :] * shifted, 0.0)
    return running

def short_back(extended, tap_table, starts_ext):
    row_count = extended.shape[0] - 8
    channel_taps = jnp.repeat(tap_table, GROUP, axis=0)
    positions = jnp.arange(row_count, dtype=jnp.int32)
    running = jnp.zeros((row_count, extended.shape[1]), jnp.float32)
    for offset in range(tap_table.shape[1]):
        shifted = extended[offset:offset + row_count].astype(jnp.float32)
        allowed = (positions >= starts_ext[offset:offset + row_count])[:, None]
        running = running + jnp.where(allowed, channel_taps[:, offset][None, :] * shifted, 0.0)
    return running

def short_taps_grad(weighted, extended, tap_table, starts):
    row_count = starts.shape[0]
    lead_rows = extended.shape[0] - row_count
    positions = jnp.arange(row_count, dtype=jnp.int32)
    weighted_f = weighted.astype(jnp.float32)
    columns = []
    for offset in range(tap_table.shape[1]):
        shifted = extended[lead_rows - offset:lead_rows - offset + row_count].astype(jnp.float32)
        allowed = (positions - offset >= starts)[:, None]
        summed = lax.optimization_barrier(jnp.sum(jnp.where(allowed, weighted_f * shifted, 0.0), axis=0))
        columns.append(lax.optimization_barrier(jnp.sum(summed.reshape(-1, GROUP), axis=1)))
    return jnp.stack(columns, axis=1)

def seq_starts(bounds):
    tile_count = bounds.shape[0]
    positions = jnp.arange(tile_count * TILE, dtype=jnp.int32)
    tile_of = positions // TILE
    within = positions - tile_of * TILE
    mine = bounds[tile_of]
    marker = jnp.where(within >= mine, tile_of * TILE + mine, -1000000).astype(jnp.int32)
    return lax.cummax(marker, axis=0)

def phase_backward(layer_input, gate_se, gate_mr, incoming, taps_se, taps_mr, starts):
    length = layer_input.shape[0]
    tile_count = length // TILE
    group_count = CHANNELS // GROUP
    scale = 1.0 / math.sqrt(length * GROUP)
    rim_rows = 8
    padded_input = jnp.pad(layer_input, ((rim_rows, 0), (0, 0)))
    se_mix = short_forward(padded_input, taps_se, starts)
    mid_acts = (layer_input.astype(jnp.float32) + gate_se.astype(jnp.float32) * se_mix).astype(jnp.bfloat16)
    taps_low = taps_mr.astype(jnp.bfloat16)
    mid_pad = jnp.pad(mid_acts, ((TILE, 0), (0, 0)))
    weighted = (gate_mr.astype(jnp.float32) * incoming.astype(jnp.float32)).astype(jnp.bfloat16)
    tile_ids = jnp.arange(tile_count, dtype=jnp.int32)

    def tile_parts(tile_num):
        anchor = tile_num * TILE
        extended = lax.dynamic_slice_in_dim(mid_pad, anchor, 2 * TILE, 0).astype(jnp.float32)
        relative = lax.dynamic_slice_in_dim(starts, anchor, TILE, 0) - anchor
        matrix, keep_mask = toeplitz_rows(taps_low, relative)
        return (anchor, extended, matrix.astype(jnp.float32), keep_mask)

    def forward_tile(tile_num):
        anchor, extended, matrix, keep_mask = tile_parts(tile_num)
        return jnp.einsum('grs,sgc->rgc', matrix, extended.reshape(2 * TILE, group_count, GROUP)).reshape(TILE, CHANNELS)
    mr_mix = lax.map(forward_tile, tile_ids).reshape(length, CHANNELS)
    grad_gate_mr = (incoming.astype(jnp.float32) * mr_mix).astype(jnp.bfloat16)

    def back_tile(tile_num):
        anchor, extended, matrix, keep_mask = tile_parts(tile_num)
        local = lax.dynamic_slice_in_dim(weighted, anchor, TILE, 0).astype(jnp.float32)
        grouped = local.reshape(TILE, group_count, GROUP)
        own_part = jnp.einsum('grs,rgc->sgc', matrix[:, :, TILE:], grouped).reshape(TILE, CHANNELS)
        prior_part = jnp.einsum('grs,rgc->sgc', matrix[:, :, :TILE], grouped).reshape(TILE, CHANNELS)
        return (own_part, prior_part, lag_grads(local, extended, keep_mask))
    own_all, prior_all, taps_all = lax.map(back_tile, tile_ids)
    prior_moved = jnp.concatenate([prior_all[1:], jnp.zeros((1, TILE, CHANNELS), jnp.float32)], axis=0)
    grad_mid = (incoming.astype(jnp.float32) + own_all.reshape(length, CHANNELS) + prior_moved.reshape(length, CHANNELS)).astype(jnp.bfloat16)
    mr_grad = lax.optimization_barrier(jnp.sum(taps_all, axis=0)) * scale
    grad_gate_se = (grad_mid.astype(jnp.float32) * se_mix).astype(jnp.bfloat16)
    weighted_se = (gate_se.astype(jnp.float32) * grad_mid.astype(jnp.float32)).astype(jnp.bfloat16)
    after_pad = jnp.pad(weighted_se, ((0, rim_rows), (0, 0)))
    starts_ext = jnp.concatenate([starts, jnp.full((rim_rows,), 2 ** 30, jnp.int32)])
    grad_x = (grad_mid.astype(jnp.float32) + short_back(after_pad, taps_se, starts_ext)).astype(jnp.bfloat16)
    se_grad = short_taps_grad(weighted_se, padded_input, taps_se, starts) * scale
    return (grad_x, grad_gate_se, grad_gate_mr, se_grad, mr_grad)

def reference(loaded, counts, destinations, bounds, se_gate, mr_gate, phase_grads, se_taps, mr_taps):
    tile_count = counts.shape[0]
    slot_ids = jnp.arange(2 * tile_count, dtype=jnp.int32)
    holding = slot_ids % 2 < counts[slot_ids // 2]
    target = jnp.where(holding, destinations, tile_count).astype(jnp.int32)
    placed = jnp.zeros((2, tile_count + 1, TILE, CHANNELS), jnp.bfloat16).at[:, target].set(loaded)
    inputs = placed[:, :tile_count].reshape(2, tile_count * TILE, CHANNELS)
    starts = seq_starts(bounds)
    results = [phase_backward(inputs[phase_id], se_gate[phase_id], mr_gate[phase_id], phase_grads[1 - phase_id], se_taps[phase_id], mr_taps[phase_id], starts) for phase_id in range(2)]
    grad_input = jnp.stack([results[0][0], results[1][0]])
    grad_se_gate = jnp.stack([results[0][1], results[1][1]])
    grad_mr_gate = jnp.stack([results[0][2], results[1][2]])
    grad_se_taps = jnp.stack([results[0][3], results[1][3]])
    grad_mr_taps = jnp.stack([results[0][4], results[1][4]])
    return (grad_input, grad_se_gate, grad_mr_gate, grad_se_taps, grad_mr_taps)
```

```python
import functools
import math

import jax
import jax.numpy as jnp
from jax import lax
from jax.experimental import pallas as pl
from jax.experimental.pallas import tpu as pltpu
from jax.sharding import PartitionSpec as P

GROUP = 16
LANES = 128
PER_BLOCK = LANES // GROUP
RIM = 8
FAR = 1 << 20
PIECES = 2
BLOCK = 512

F32 = jnp.float32
BF16 = jnp.bfloat16


def from_behind(block, axis, distance):
    devices = range(lax.axis_size(axis))
    route = [(i - distance, i) for i in devices if i - distance in devices]
    return lax.ppermute(block, axis, route)


def partner(value, axis, mask):
    pairs = [(source, source ^ mask) for source in range(lax.axis_size(axis))]
    return lax.ppermute(value, axis, pairs)


def grid_of(rows, which):
    return lax.broadcasted_iota(jnp.int32, (rows, rows), which)


def same_tile(out_row, in_row, bound):
    return (out_row >= in_row) & ((out_row < bound) | (in_row >= bound))


def tile_before(out_row, in_row, bound, earlier, rows):
    return (out_row < in_row) & (out_row < bound) & ((earlier >= rows) | (in_row >= earlier))


def as_mask(flags, dtype):
    return jnp.where(flags, 1.0, 0.0).astype(F32).astype(dtype)


def room_of(row, bound, earlier, rows):
    before = jnp.where(earlier < rows, row + (rows - earlier), FAR)
    return jnp.where(row >= bound, row - bound, before)


def rolled(line, rows):
    return pltpu.roll(jnp.broadcast_to(line, (rows, rows)), 0, 1, stride=1, stride_axis=0)


def lanes(start):
    return pl.ds(start, LANES)


def middle_kernel(sc, slot, arrived, rim_a, rim_b, gate, taps, hr, x_out, mid_out, mix_out, own_out, ext, room, mask):
    rows = slot.shape[0]
    earlier, bound, has_own = sc[0], sc[1], sc[3]

    @pl.when(pl.program_id(0) == 0)
    def _():
        row = lax.broadcasted_iota(jnp.int32, (rows, LANES), 0)
        room[...] = room_of(row, bound, earlier, rows)
        mask[...] = as_mask(same_tile(grid_of(rows, 0), grid_of(rows, 1), bound), BF16)

    lane_group = lax.broadcasted_iota(jnp.int32, (rows, LANES), 1) // GROUP
    for block in range(slot.shape[1] // LANES):
        at = lanes(block * LANES)
        x = jnp.where(has_own > 0, slot[:, at].astype(F32), arrived[:, at].astype(F32))
        rim = rim_a[:, at].astype(F32) + rim_b[:, at].astype(F32)
        x_out[:, at] = x.astype(BF16)
        ext[block, :RIM] = rim
        ext[block, RIM:] = x
        mix = jnp.zeros((rows, LANES), F32)
        for lag in range(taps.shape[0] - 1):
            shifted = ext[block, RIM - lag : RIM - lag + rows]
            mix = mix + jnp.where(room[...] >= lag, taps[lag : lag + 1, at] * shifted, 0.0)
        mix_out[:, at] = mix
        mid = (x + gate[:, at].astype(F32) * mix).astype(BF16)
        mid_out[:, at] = mid
        own = jnp.zeros((rows, LANES), F32)
        for group in range(PER_BLOCK):
            at_group = block * PER_BLOCK + group
            matrix = rolled(hr[at_group : at_group + 1], rows).astype(BF16) * mask[...]
            product = jnp.dot(matrix, mid, preferred_element_type=F32)
            own = jnp.where(lane_group == group, product, own)
        own_out[:, at] = own


def middle(sc, slot, arrived, rim_a, rim_b, gate, taps, hr):
    rows, channels = gate.shape
    wide = lambda height: pl.BlockSpec((height, BLOCK), lambda i: (0, i))
    shape = lambda dtype: jax.ShapeDtypeStruct((rows, channels), dtype)
    return pl.pallas_call(
        middle_kernel,
        grid=(channels // BLOCK,),
        in_specs=[
            pl.BlockSpec(memory_space=pltpu.SMEM),
            wide(rows),
            wide(rows),
            wide(RIM),
            wide(RIM),
            wide(rows),
            wide(taps.shape[0]),
            pl.BlockSpec((BLOCK // GROUP, rows), lambda i: (i, 0)),
        ],
        out_specs=[wide(rows)] * 4,
        out_shape=[shape(BF16), shape(BF16), shape(F32), shape(F32)],
        scratch_shapes=[
            pltpu.VMEM((BLOCK // LANES, rows + RIM, LANES), F32),
            pltpu.VMEM((rows, LANES), jnp.int32),
            pltpu.VMEM((rows, rows), BF16),
        ],
        compiler_params=pltpu.CompilerParams(vmem_limit_bytes=40 << 20),
        cost_estimate=pl.CostEstimate(flops=2 * rows * rows * channels, bytes_accessed=18 * rows * channels, transcendentals=0),
    )(sc, slot, arrived, rim_a, rim_b, gate, taps, hr)


def back_kernel(
    shift, sc, weighted, after, incoming, mid, x, rim_a, rim_b, mix, gate, h,
    mid_grad, gate_grad, wse_out, lag_out, se_out,
    ext, room, mask_own, mask_next, lag_own, lag_next, flip,
):
    rows = weighted.shape[0]
    step = pl.program_id(0)
    earlier, bound, later = sc[0], sc[1], sc[2]

    @pl.when(step == 0)
    def _():
        row = lax.broadcasted_iota(jnp.int32, (rows, LANES), 0)
        room[...] = room_of(row, bound, earlier, rows)
        source, target = grid_of(rows, 0), grid_of(rows, 1)
        mask_own[...] = as_mask(same_tile(target, source, bound), BF16)
        mask_next[...] = as_mask(tile_before(target, source, later, bound, rows), BF16)
        mirrored = rows - 1 - source
        lag_own[...] = as_mask(same_tile(target, mirrored, bound), F32)
        lag_next[...] = as_mask(tile_before(target, mirrored, later, bound, rows), F32)
        flip[...] = as_mask(mirrored == target, BF16)
        se_out[...] = jnp.zeros_like(se_out)

    lane_group = lax.broadcasted_iota(jnp.int32, (rows, LANES), 1) // GROUP
    one_row = lax.broadcasted_iota(jnp.int32, (1, LANES), 1) // GROUP
    channel = grid_of(LANES, 0) // GROUP
    column = grid_of(LANES, 1)
    for block in range(weighted.shape[1] // LANES):
        at = lanes(block * LANES)
        pair = jnp.concatenate([weighted[:, at], after[:, at]], axis=0)
        total = jnp.zeros((rows, LANES), F32)
        for group in range(PER_BLOCK):
            at_group = block * PER_BLOCK + group
            circle = rolled(h[at_group : at_group + 1], rows).astype(BF16)
            matrix = jnp.concatenate([circle * mask_own[...], circle * mask_next[...]], axis=1)
            product = jnp.dot(matrix, pair, preferred_element_type=F32)
            total = jnp.where(lane_group == group, product, total)
        grad = (incoming[:, at].astype(F32) + total).astype(BF16)
        mid_grad[:, at] = grad
        grad_wide = grad.astype(F32)
        gate_grad[:, at] = (grad_wide * mix[:, at]).astype(BF16)
        wse = (gate[:, at].astype(F32) * grad_wide).astype(BF16)
        wse_out[:, at] = wse
        wse_wide = wse.astype(F32)
        ext[block, :RIM] = rim_a[:, at].astype(F32) + rim_b[:, at].astype(F32)
        ext[block, RIM:] = x[:, at].astype(F32)
        sums = []
        for lag in range(se_out.shape[0] - 1):
            shifted = ext[block, RIM - lag : RIM - lag + rows]
            sums.append(jnp.sum(jnp.where(room[...] >= lag, wse_wide * shifted, 0.0), axis=0, keepdims=True))
        sums.append(jnp.zeros((1, LANES), F32))
        place = shift + (step * (weighted.shape[1] // LANES) + block) * PER_BLOCK
        spread = as_mask(column == channel + place, F32)
        se_out[...] += jnp.dot(
            jnp.concatenate(sums, axis=0), spread, preferred_element_type=F32, precision=lax.Precision.HIGHEST
        )
        mirrored_mid = jnp.dot(flip[...], mid[:, at], preferred_element_type=F32).astype(BF16)
        lags = []
        for group in range(PER_BLOCK):
            chosen = mirrored_mid * as_mask(one_row == group, BF16)
            products = lax.dot_general(chosen, pair, (((1,), (1,)), ((), ())), preferred_element_type=F32)
            kept = products[:, :rows] * lag_own[...] + products[:, rows:] * lag_next[...]
            kept = pltpu.roll(kept, 1, 1, stride=1, stride_axis=0)
            lags.append(jnp.sum(kept, axis=0, keepdims=True))
        lag_out[block * PER_BLOCK : (block + 1) * PER_BLOCK] = jnp.concatenate(lags, axis=0)


def back(piece, pieces, sc, weighted, after, incoming, mid, x, rim_a, rim_b, mix, gate, h):
    rows, channels = weighted.shape
    part = channels // pieces
    groups = part // GROUP
    first = piece * part // BLOCK
    full = lambda height: pl.BlockSpec((height, BLOCK), lambda i: (0, first + i))
    own = lambda height: pl.BlockSpec((height, BLOCK), lambda i: (0, i))
    shape = lambda dtype: jax.ShapeDtypeStruct((rows, part), dtype)
    square = lambda dtype: pltpu.VMEM((rows, rows), dtype)
    return pl.pallas_call(
        functools.partial(back_kernel, (piece * groups) % LANES),
        grid=(part // BLOCK,),
        in_specs=[
            pl.BlockSpec(memory_space=pltpu.SMEM),
            full(rows),
            own(rows),
            full(rows),
            full(rows),
            full(rows),
            full(RIM),
            full(RIM),
            full(rows),
            full(rows),
            pl.BlockSpec((BLOCK // GROUP, rows), lambda i: (first + i, 0)),
        ],
        out_specs=[
            own(rows),
            own(rows),
            own(rows),
            pl.BlockSpec((BLOCK // GROUP, rows), lambda i: (i, 0)),
            pl.BlockSpec((RIM, LANES), lambda i: (0, 0)),
        ],
        out_shape=[
            shape(BF16),
            shape(BF16),
            shape(BF16),
            jax.ShapeDtypeStruct((groups, rows), F32),
            jax.ShapeDtypeStruct((RIM, LANES), F32),
        ],
        scratch_shapes=[
            pltpu.VMEM((BLOCK // LANES, rows + RIM, LANES), F32),
            pltpu.VMEM((rows, LANES), jnp.int32),
            square(BF16),
            square(BF16),
            square(F32),
            square(F32),
            square(BF16),
        ],
        compiler_params=pltpu.CompilerParams(vmem_limit_bytes=40 << 20),
        cost_estimate=pl.CostEstimate(flops=8 * rows * rows * part, bytes_accessed=22 * rows * part, transcendentals=0),
    )(sc, weighted, after, incoming, mid, x, rim_a, rim_b, mix, gate, h)


def input_kernel(sc, *refs):
    pieces = (len(refs) - 5) // 2
    grads, wses = refs[:pieces], refs[pieces : 2 * pieces]
    rim, taps, out, ext, room = refs[2 * pieces :]
    rows = out.shape[0]
    bound, later = sc[1], sc[2]
    step = pl.program_id(0)

    @pl.when(step == 0)
    def _():
        row = lax.broadcasted_iota(jnp.int32, (rows, LANES), 0)
        room[:rows] = room_of(row, bound, sc[0], rows)
        rim_row = lax.broadcasted_iota(jnp.int32, (RIM, LANES), 0)
        room[rows:] = room_of(rim_row, later, bound, rows)

    per = pl.num_programs(0) // pieces
    for piece in range(pieces):

        @pl.when((step >= piece * per) & (step < (piece + 1) * per))
        def _(piece=piece):
            for block in range(out.shape[1] // LANES):
                at = lanes(block * LANES)
                ext[block, :rows] = wses[piece][:, at].astype(F32)
                ext[block, rows:] = rim[:, at].astype(F32)
                total = grads[piece][:, at].astype(F32)
                for lag in range(taps.shape[0] - 1):
                    shifted = ext[block, lag : lag + rows]
                    total = total + jnp.where(room[lag : lag + rows] >= lag, taps[lag : lag + 1, at] * shifted, 0.0)
                out[:, at] = total.astype(BF16)


def input_grad(sc, grads, wses, rim, taps):
    pieces = len(grads)
    rows = grads[0].shape[0]
    channels = rim.shape[1]
    per = channels // BLOCK // pieces
    wide = lambda height: pl.BlockSpec((height, BLOCK), lambda i: (0, i))
    held = [
        pl.BlockSpec((rows, BLOCK), lambda i, piece=piece: (0, jnp.clip(i - piece * per, 0, per - 1)))
        for piece in range(pieces)
    ]
    return pl.pallas_call(
        input_kernel,
        grid=(channels // BLOCK,),
        in_specs=[pl.BlockSpec(memory_space=pltpu.SMEM), *held, *held, wide(RIM), wide(taps.shape[0])],
        out_specs=wide(rows),
        out_shape=jax.ShapeDtypeStruct((rows, channels), BF16),
        scratch_shapes=[
            pltpu.VMEM((BLOCK // LANES, rows + RIM, LANES), F32),
            pltpu.VMEM((rows + RIM, LANES), jnp.int32),
        ],
        compiler_params=pltpu.CompilerParams(vmem_limit_bytes=40 << 20),
        cost_estimate=pl.CostEstimate(flops=14 * rows * channels, bytes_accessed=6 * rows * channels, transcendentals=0),
    )(sc, *grads, *wses, rim, taps)


def gate_kernel(sc, prior, own, incoming, hr, *rest):
    out, mask = rest[-2:]
    rows = prior.shape[0]

    @pl.when(pl.program_id(0) == 0)
    def _():
        mask[...] = as_mask(tile_before(grid_of(rows, 0), grid_of(rows, 1), sc[1], sc[0], rows), BF16)

    lane_group = lax.broadcasted_iota(jnp.int32, (rows, LANES), 1) // GROUP
    for block in range(prior.shape[1] // LANES):
        at = lanes(block * LANES)
        total = jnp.zeros((rows, LANES), F32)
        for group in range(PER_BLOCK):
            at_group = block * PER_BLOCK + group
            matrix = rolled(hr[at_group : at_group + 1], rows).astype(BF16) * mask[...]
            product = jnp.dot(matrix, prior[:, at], preferred_element_type=F32)
            total = jnp.where(lane_group == group, product, total)
        out[:, at] = (incoming[:, at].astype(F32) * (own[:, at] + total)).astype(BF16)


def gate_grad(piece, pieces, sc, prior, own, incoming, hr, held):
    rows, channels = own.shape
    part = channels // pieces
    first = piece * part // BLOCK
    full = lambda: pl.BlockSpec((rows, BLOCK), lambda i: (0, first + i))
    return pl.pallas_call(
        gate_kernel,
        grid=(part // BLOCK,),
        in_specs=[
            pl.BlockSpec(memory_space=pltpu.SMEM),
            pl.BlockSpec((rows, BLOCK), lambda i: (0, i)),
            full(),
            full(),
            pl.BlockSpec((BLOCK // GROUP, rows), lambda i: (first + i, 0)),
        ]
        + [pl.BlockSpec(memory_space=pl.ANY)] * len(held),
        out_specs=full(),
        out_shape=jax.ShapeDtypeStruct((rows, channels), BF16),
        scratch_shapes=[pltpu.VMEM((rows, rows), BF16)],
        input_output_aliases={5: 0} if held else {},
        compiler_params=pltpu.CompilerParams(vmem_limit_bytes=40 << 20),
        cost_estimate=pl.CostEstimate(flops=2 * rows * rows * part, bytes_accessed=10 * rows * part, transcendentals=0),
    )(sc, prior, own, incoming, hr, *held)


def body(loaded, counts, destinations, bounds, se_gate, mr_gate, phase_grads, se_taps, mr_taps):
    ctx_count = lax.axis_size("ctx")
    shard_index = lax.axis_index("ctx")
    slots = loaded[0]
    rows, channels = slots.shape[1], slots.shape[2]
    group_count = channels // GROUP
    part = channels // PIECES
    held_count = counts[0]
    first_dest, second_dest = destinations[0], destinations[1]
    own_tile = (held_count >= 1) & (first_dest == shard_index)
    send_first = (held_count >= 1) & (first_dest == shard_index + 1)
    send_second = (held_count >= 2) & (second_dest == shard_index + 1)

    incoming = partner(phase_grads[0], "pipe", 1)
    outgoing = lax.dynamic_index_in_dim(slots, jnp.where(send_first, 0, 1), 0, False)
    arrived = from_behind(outgoing, "ctx", 1)

    nothing = jnp.zeros((), BF16)
    tail_own = jnp.where(own_tile, slots[0, rows - RIM :], nothing)
    tail_sent = jnp.where(send_first | send_second, outgoing[rows - RIM :], nothing)
    rim_a = from_behind(tail_own, "ctx", 1)
    rim_b = from_behind(tail_sent, "ctx", 2)

    tile_total = bounds.shape[0]

    def bound_at(tile_num):
        inside = (tile_num >= 0) & (tile_num < tile_total)
        return jnp.where(inside, bounds[jnp.clip(tile_num, 0, tile_total - 1)], rows)

    sc = jnp.stack(
        [bound_at(shard_index - 1), bound_at(shard_index), bound_at(shard_index + 1), own_tile.astype(jnp.int32)]
    ).astype(jnp.int32)
    taps_low = mr_taps[0].astype(BF16).astype(F32)
    taps_back = jnp.roll(taps_low[:, ::-1], 1, axis=1)
    taps_se = jnp.repeat(jnp.pad(se_taps[0].T, ((0, 1), (0, 0))), GROUP, axis=1)
    gate_se = se_gate[0]

    weighted = (mr_gate[0].astype(F32) * incoming.astype(F32)).astype(BF16)
    after = [from_behind(weighted[:, q * part : (q + 1) * part], "ctx", -1) for q in range(PIECES)]

    layer_input, mid, se_mix, mr_own = middle(sc, slots[0], arrived, rim_a, rim_b, gate_se, taps_se, taps_back)
    prior = [from_behind(mid[:, q * part : (q + 1) * part], "ctx", 1) for q in range(PIECES)]

    done = [
        back(q, PIECES, sc, weighted, after[q], incoming, mid, layer_input, rim_a, rim_b, se_mix, gate_se, taps_low)
        for q in range(PIECES)
    ]
    mid_grads, gate_grads, wses, lags, se_sums = zip(*done)
    rim_next = from_behind(jnp.concatenate([wse[:RIM] for wse in wses], axis=1), "ctx", -1)
    grad_x = input_grad(sc, mid_grads, wses, rim_next, taps_se)
    grad_gate_se = jnp.concatenate(gate_grads, axis=1)

    grad_gate_mr = ()
    for q in range(PIECES):
        grad_gate_mr = (gate_grad(q, PIECES, sc, prior[q], mr_own, incoming, taps_back, grad_gate_mr),)
    grad_gate_mr = grad_gate_mr[0]

    total = jnp.concatenate([*lags, *se_sums], axis=0)
    mask = ctx_count // 2
    while mask:
        total = total + partner(total, "ctx", mask)
        mask //= 2
    scale = 1.0 / math.sqrt(ctx_count * rows * GROUP)
    total = total * scale
    mr_total = total[:group_count]
    windows = max(group_count // LANES, 1)
    se_total = total[group_count:].reshape(windows, PIECES // windows, RIM, LANES).sum(axis=1)
    se_total = se_total.transpose(0, 2, 1).reshape(group_count, RIM)[:, : se_taps.shape[2]]
    return (grad_x[None], grad_gate_se[None], grad_gate_mr[None], se_total[None], mr_total[None])


def solution(mesh):
    return jax.shard_map(
        body,
        mesh=mesh,
        in_specs=(
            P("pipe", "ctx", None, None),
            P("ctx"),
            P("ctx"),
            P(),
            P("pipe", "ctx", None),
            P("pipe", "ctx", None),
            P("pipe", "ctx", None),
            P("pipe", None, None),
            P("pipe", None, None),
        ),
        out_specs=(
            P("pipe", "ctx", None),
            P("pipe", "ctx", None),
            P("pipe", "ctx", None),
            P("pipe", None, None),
            P("pipe", None, None),
        ),
        check_vma=False,
    )
```

```python
import functools
import math

import jax
import jax.numpy as jnp
from jax import lax
from jax.experimental import pallas as pl
from jax.experimental.pallas import tpu as pltpu
from jax.sharding import PartitionSpec as P

GROUP = 16
LANES = 128
PER_BLOCK = LANES // GROUP
RIM = 8
FAR = 1 << 20
PIECES = 2
BLOCK = 2048

F32 = jnp.float32
BF16 = jnp.bfloat16


def from_behind(block, axis, distance):
    devices = range(lax.axis_size(axis))
    route = [(i - distance, i) for i in devices if i - distance in devices]
    return lax.ppermute(block, axis, route)


def partner(value, axis, mask):
    pairs = [(source, source ^ mask) for source in range(lax.axis_size(axis))]
    return lax.ppermute(value, axis, pairs)


def exchange_order(count):
    masks = [1 << bit for bit in range(count.bit_length() - 1)]
    return masks[1:] + masks[:1]


def grid_of(rows, which):
    return lax.broadcasted_iota(jnp.int32, (rows, rows), which)


def same_tile(out_row, in_row, bound):
    return (out_row >= in_row) & ((out_row < bound) | (in_row >= bound))


def tile_before(out_row, in_row, bound, earlier, rows):
    return (out_row < in_row) & (out_row < bound) & ((earlier >= rows) | (in_row >= earlier))


def as_mask(flags, dtype):
    return jnp.where(flags, 1.0, 0.0).astype(F32).astype(dtype)


def room_of(row, bound, earlier, rows):
    before = jnp.where(earlier < rows, row + (rows - earlier), FAR)
    return jnp.where(row >= bound, row - bound, before)


def rolled(line, rows):
    return pltpu.roll(jnp.broadcast_to(line, (rows, rows)), 0, 1, stride=1, stride_axis=0)


def lanes(start):
    return pl.ds(start, LANES)


def bounds_near(bounds, rows):
    count = bounds.shape[0]
    shard = lax.axis_index("ctx")
    near = []
    for tile in (shard - 1, shard, shard + 1):
        bound = bounds[jnp.clip(tile, 0, count - 1)]
        near.append(jnp.where((tile >= 0) & (tile < count), bound, rows))
    return near


def holds_own(counts, destinations):
    return (counts[0] >= 1) & (destinations[0] == lax.axis_index("ctx"))


SCALARS = pl.BlockSpec(memory_space=pltpu.SMEM)
FREE = pl.CostEstimate(flops=1, bytes_accessed=1, transcendentals=0)
ROOM = pltpu.CompilerParams(vmem_limit_bytes=40 << 20)


def pick_kernel(counts, destinations, slot, first, *outs):
    *pieces, sent_tail = outs
    rows = slot.shape[0]
    shard = lax.axis_index("ctx")
    sends = ((counts[0] >= 1) & (destinations[0] == shard + 1)) | ((counts[0] >= 2) & (destinations[1] == shard + 1))
    picked = slot[...]
    own = jnp.where(holds_own(counts, destinations), first[...].astype(F32), 0.0)[-RIM:].astype(BF16)
    for number, piece in enumerate(pieces):

        @pl.when(pl.program_id(0) == number)
        def _(piece=piece):
            piece[:rows] = picked
            piece[rows:] = own

    sent_tail[...] = jnp.where(sends, picked[-2 * RIM :].astype(F32), 0.0)[-RIM:].astype(BF16)


def pick_outgoing(counts, destinations, loaded):
    rows, channels = loaded.shape[2:]
    width = channels // PIECES
    shape = lambda height, size: jax.ShapeDtypeStruct((height, size), loaded.dtype)
    return pl.pallas_call(
        pick_kernel,
        grid_spec=pltpu.PrefetchScalarGridSpec(
            num_scalar_prefetch=2,
            grid=(PIECES,),
            in_specs=[
                pl.BlockSpec((None, None, rows, width), lambda i, held, _: (0, jnp.where(held[0] == 2, 1, 0), 0, i)),
                pl.BlockSpec((None, None, 2 * RIM, width), lambda i, *_: (0, 0, rows // (2 * RIM) - 1, i)),
            ],
            out_specs=[pl.BlockSpec((rows + RIM, width), lambda i, *_: (0, 0))] * PIECES
            + [pl.BlockSpec((RIM, width), lambda i, *_: (0, i))],
        ),
        out_shape=[shape(rows + RIM, width)] * PIECES + [shape(RIM, channels)],
        cost_estimate=FREE,
    )(counts, destinations, loaded, loaded)


def taps_kernel(mr, se, low, mirrored, spread):
    groups, count = mr.shape
    rounded = mr[...].astype(BF16)
    low[...] = rounded.astype(F32)
    mirror = as_mask(lax.rem(grid_of(count, 0) + grid_of(count, 1), count) == 0, BF16)
    mirrored[...] = jnp.dot(rounded, mirror, preferred_element_type=F32)
    taps = se.shape[1]
    group = lax.broadcasted_iota(jnp.int32, (PER_BLOCK, LANES), 0)
    owner = lax.broadcasted_iota(jnp.int32, (PER_BLOCK, LANES), 1) // GROUP
    widen = as_mask(group == owner, F32)
    for block in range(groups // PER_BLOCK):
        part = se[block * PER_BLOCK : (block + 1) * PER_BLOCK]
        for tap in range(taps):
            line = jnp.sum(part[:, tap : tap + 1] * widen, axis=0, keepdims=True)
            spread[tap : tap + 1, lanes(block * LANES)] = line
    spread[taps:] = jnp.zeros((spread.shape[0] - taps, spread.shape[1]), F32)


def taps_forms(mr_taps, se_taps):
    groups, count = mr_taps.shape
    return pl.pallas_call(
        taps_kernel,
        out_shape=[
            jax.ShapeDtypeStruct((groups, count), F32),
            jax.ShapeDtypeStruct((groups, count), F32),
            jax.ShapeDtypeStruct((RIM, groups * GROUP), F32),
        ],
        cost_estimate=FREE,
    )(mr_taps, se_taps)


def filtered(matrix_of, values, rows):
    lane_group = lax.broadcasted_iota(jnp.int32, (rows, LANES), 1) // GROUP
    total = jnp.zeros((rows, LANES), F32)
    for group in range(PER_BLOCK):
        product = jnp.dot(matrix_of(group), values, preferred_element_type=F32)
        total = jnp.where(lane_group == group, product, total)
    return total


def own_back_kernel(bounds, weighted, incoming, low, out, mask):
    rows = weighted.shape[0]
    _, bound, _ = bounds_near(bounds, rows)

    @pl.when(pl.program_id(0) == 0)
    def _():
        mask[...] = as_mask(same_tile(grid_of(rows, 1), grid_of(rows, 0), bound), BF16)

    for block in range(weighted.shape[1] // LANES):
        at = lanes(block * LANES)

        def matrix_of(group):
            line = block * PER_BLOCK + group
            return rolled(low[line : line + 1], rows).astype(BF16) * mask[...]

        out[:, at] = incoming[:, at].astype(F32) + filtered(matrix_of, weighted[:, at], rows)


def own_back(bounds, weighted, incoming, low):
    rows, channels = weighted.shape
    wide = lambda height: pl.BlockSpec((height, BLOCK), lambda i: (0, i))
    return pl.pallas_call(
        own_back_kernel,
        grid=(channels // BLOCK,),
        in_specs=[SCALARS, wide(rows), wide(rows), pl.BlockSpec((BLOCK // GROUP, rows), lambda i: (i, 0))],
        out_specs=wide(rows),
        out_shape=jax.ShapeDtypeStruct((rows, channels), F32),
        scratch_shapes=[pltpu.VMEM((rows, rows), BF16)],
        compiler_params=ROOM,
        cost_estimate=FREE,
    )(bounds, weighted, incoming, low)


def next_back_kernel(bounds, after, base, gate, low, mid_grad, wse, mask):
    rows = after.shape[0]
    _, bound, later = bounds_near(bounds, rows)

    @pl.when(pl.program_id(0) == 0)
    def _():
        mask[...] = as_mask(tile_before(grid_of(rows, 1), grid_of(rows, 0), later, bound, rows), BF16)

    for block in range(after.shape[1] // LANES):
        at = lanes(block * LANES)

        def matrix_of(group):
            line = block * PER_BLOCK + group
            return rolled(low[line : line + 1], rows).astype(BF16) * mask[...]

        grad = (base[:, at] + filtered(matrix_of, after[:, at], rows)).astype(BF16)
        mid_grad[:, at] = grad
        wse[:, at] = (gate[:, at].astype(F32) * grad.astype(F32)).astype(BF16)


def next_back(bounds, after, base, gate, low):
    rows, channels = after.shape
    wide = lambda height: pl.BlockSpec((height, BLOCK), lambda i: (0, i))
    return pl.pallas_call(
        next_back_kernel,
        grid=(channels // BLOCK,),
        in_specs=[
            SCALARS,
            wide(rows),
            wide(rows),
            wide(rows),
            pl.BlockSpec((BLOCK // GROUP, rows), lambda i: (i, 0)),
        ],
        out_specs=[wide(rows)] * 2,
        out_shape=[jax.ShapeDtypeStruct((rows, channels), BF16)] * 2,
        scratch_shapes=[pltpu.VMEM((rows, rows), BF16)],
        compiler_params=ROOM,
        cost_estimate=FREE,
    )(bounds, after, base, gate, low)


def middle_kernel(shift, bounds, counts, destinations, slot, arrived, rim, gate, taps, grad, wse, *rest):
    mid_out, gate_grad, se_out, ext, room, spread = rest[-6:]
    rows = slot.shape[0]
    step = pl.program_id(0)
    earlier, bound, _ = bounds_near(bounds, rows)
    own_here = holds_own(counts, destinations)

    @pl.when(step == 0)
    def _():
        row = lax.broadcasted_iota(jnp.int32, (rows, LANES), 0)
        room[...] = room_of(row, bound, earlier, rows)
        se_out[...] = jnp.zeros_like(se_out)
        spread[...] = as_mask(grid_of(LANES, 0) // GROUP == grid_of(LANES, 1), BF16)

    blocks = slot.shape[1] // LANES
    thirds = []
    for block in range(blocks):
        at = lanes(block * LANES)
        x = jnp.where(own_here, slot[:, at].astype(F32), arrived[:rows, at].astype(F32))
        ext[block, :RIM] = arrived[rows:, at].astype(F32) + rim[:, at].astype(F32)
        ext[block, RIM:] = x
        mix = jnp.zeros((rows, LANES), F32)
        wide_wse = wse[:, at].astype(F32)
        sums = []
        for lag in range(taps.shape[0] - 1):
            kept = jnp.where(room[...] >= lag, ext[block, RIM - lag : RIM - lag + rows], 0.0)
            mix = mix + taps[lag : lag + 1, at] * kept
            sums.append(jnp.sum(wide_wse * kept, axis=0, keepdims=True))
        sums.append(jnp.zeros((1, LANES), F32))
        mid_out[:, at] = (x + gate[:, at].astype(F32) * mix).astype(BF16)
        gate_grad[:, at] = (grad[:, at].astype(F32) * mix).astype(BF16)
        left = jnp.concatenate(sums, axis=0)
        for _ in range(3):
            term = left.astype(BF16).astype(F32)
            thirds.append(term)
            left = left - term
    parts = jnp.dot(jnp.concatenate(thirds, axis=0).astype(BF16), spread[...], preferred_element_type=F32)
    gathered = jnp.zeros((RIM, LANES), F32)
    for block in range(blocks):
        first = 3 * RIM * block
        part = parts[first : first + RIM] + parts[first + RIM : first + 2 * RIM] + parts[first + 2 * RIM : first + 3 * RIM]
        gathered = gathered + (pltpu.roll(part, block * PER_BLOCK, 1) if block else part)
    place = lax.rem(shift + step * blocks * PER_BLOCK, LANES)
    se_out[...] += pltpu.roll(gathered, place, 1)


def middle(piece, bounds, counts, destinations, loaded, arrived, rim, gate, taps, grad, wse, held):
    rows, channels = gate.shape
    part = channels // PIECES
    groups = channels // GROUP
    first = piece * part // BLOCK
    full = lambda height: pl.BlockSpec((height, BLOCK), lambda i: (0, first + i))
    own = lambda height: pl.BlockSpec((height, BLOCK), lambda i: (0, i))
    return pl.pallas_call(
        functools.partial(middle_kernel, (piece * groups // PIECES) % LANES),
        grid=(part // BLOCK,),
        in_specs=[
            SCALARS,
            SCALARS,
            SCALARS,
            pl.BlockSpec((None, None, rows, BLOCK), lambda i: (0, 0, 0, first + i)),
            own(rows + RIM),
            full(RIM),
            full(rows),
            full(taps.shape[0]),
            full(rows),
            full(rows),
        ]
        + [pl.BlockSpec(memory_space=pl.ANY)] * len(held),
        out_specs=[own(rows), full(rows), pl.BlockSpec((RIM, LANES), lambda i: (0, 0))],
        out_shape=[
            jax.ShapeDtypeStruct((rows, part), BF16),
            jax.ShapeDtypeStruct((rows, channels), BF16),
            jax.ShapeDtypeStruct((RIM, LANES), F32),
        ],
        scratch_shapes=[
            pltpu.VMEM((BLOCK // LANES, rows + RIM, LANES), F32),
            pltpu.VMEM((rows, LANES), jnp.int32),
            pltpu.VMEM((LANES, LANES), BF16),
        ],
        input_output_aliases={10: 1} if held else {},
        compiler_params=ROOM,
        cost_estimate=FREE,
    )(bounds, counts, destinations, loaded, arrived, rim, gate, taps, grad, wse, *held)


def lag_kernel(bounds, mid, weighted, after, *rest):
    out, lag_own, lag_next, flip, flipped = rest[-5:]
    rows = mid.shape[0]
    _, bound, later = bounds_near(bounds, rows)

    @pl.when(pl.program_id(0) == 0)
    def _():
        target = grid_of(rows, 1)
        mirrored = rows - 1 - grid_of(rows, 0)
        lag_own[...] = as_mask(same_tile(target, mirrored, bound), F32)
        lag_next[...] = as_mask(tile_before(target, mirrored, later, bound, rows), F32)
        flip[...] = as_mask(mirrored == target, BF16)

    one_row = lax.broadcasted_iota(jnp.int32, (1, LANES), 1) // GROUP
    for block in range(mid.shape[1] // LANES):
        flipped[block] = jnp.dot(flip[...], mid[:, lanes(block * LANES)], preferred_element_type=F32).astype(BF16)
    for block in range(mid.shape[1] // LANES):
        at = lanes(block * LANES)
        pair = jnp.concatenate([weighted[:, at], after[:, at]], axis=0).T
        mirrored_mid = flipped[block]
        lags = []
        for group in range(PER_BLOCK):
            chosen = mirrored_mid * as_mask(one_row == group, BF16)
            products = jnp.dot(chosen, pair, preferred_element_type=F32)
            kept = products[:, :rows] * lag_own[...] + products[:, rows:] * lag_next[...]
            kept = pltpu.roll(kept, 1, 1, stride=1, stride_axis=0)
            lags.append(jnp.sum(kept, axis=0, keepdims=True))
        out[block * PER_BLOCK : (block + 1) * PER_BLOCK] = jnp.concatenate(lags, axis=0)


def lag_grads(piece, bounds, mid, weighted, after, held):
    rows, channels = weighted.shape
    part = channels // PIECES
    first = piece * part // BLOCK
    full = lambda height: pl.BlockSpec((height, BLOCK), lambda i: (0, first + i))
    square = lambda dtype: pltpu.VMEM((rows, rows), dtype)
    return pl.pallas_call(
        lag_kernel,
        grid=(part // BLOCK,),
        in_specs=[SCALARS, pl.BlockSpec((rows, BLOCK), lambda i: (0, i)), full(rows), full(rows)]
        + [pl.BlockSpec(memory_space=pl.ANY)] * len(held),
        out_specs=pl.BlockSpec((BLOCK // GROUP, rows), lambda i: (first + i, 0)),
        out_shape=jax.ShapeDtypeStruct((channels // GROUP, rows), F32),
        scratch_shapes=[square(F32), square(F32), square(BF16), pltpu.VMEM((BLOCK // LANES, rows, LANES), BF16)],
        input_output_aliases={4: 0} if held else {},
        compiler_params=ROOM,
        cost_estimate=FREE,
    )(bounds, mid, weighted, after, *held)


def input_kernel(bounds, grad, wse, taps, out, ext, room):
    rows = out.shape[0]
    earlier, bound, _ = bounds_near(bounds, rows)

    @pl.when(pl.program_id(0) == 0)
    def _():
        row = lax.broadcasted_iota(jnp.int32, (rows, LANES), 0)
        room[:rows] = room_of(row, bound, earlier, rows)
        room[rows:] = jnp.zeros((RIM, LANES), jnp.int32)

    for block in range(out.shape[1] // LANES):
        at = lanes(block * LANES)
        ext[block, :rows] = wse[:, at].astype(F32)
        ext[block, rows:] = jnp.zeros((RIM, LANES), F32)
        total = grad[:, at].astype(F32)
        for lag in range(taps.shape[0] - 1):
            shifted = ext[block, lag : lag + rows]
            total = total + jnp.where(room[lag : lag + rows] >= lag, taps[lag : lag + 1, at] * shifted, 0.0)
        out[:, at] = total.astype(BF16)


def input_grad(bounds, grad, wse, taps):
    rows, channels = grad.shape
    wide = lambda height: pl.BlockSpec((height, BLOCK), lambda i: (0, i))
    return pl.pallas_call(
        input_kernel,
        grid=(channels // BLOCK,),
        in_specs=[SCALARS, wide(rows), wide(rows), wide(taps.shape[0])],
        out_specs=wide(rows),
        out_shape=jax.ShapeDtypeStruct((rows, channels), BF16),
        scratch_shapes=[
            pltpu.VMEM((BLOCK // LANES, rows + RIM, LANES), F32),
            pltpu.VMEM((rows + RIM, LANES), jnp.int32),
        ],
        compiler_params=ROOM,
        cost_estimate=FREE,
    )(bounds, grad, wse, taps)


def rim_kernel(rows, bounds, grad, wse, rim, taps, held, out, ext):
    del held
    some = out.shape[0]
    earlier, bound, later = bounds_near(bounds, rows)
    row = lax.broadcasted_iota(jnp.int32, (some, out.shape[1]), 0) + (rows - some)
    rim_row = lax.broadcasted_iota(jnp.int32, (RIM, out.shape[1]), 0)
    ext[0, :some] = wse[...].astype(F32)
    ext[0, some:] = rim[...].astype(F32)
    ext[1, :some] = room_of(row, bound, earlier, rows).astype(F32)
    ext[1, some:] = room_of(rim_row, later, bound, rows).astype(F32)
    total = grad[...].astype(F32)
    for lag in range(taps.shape[0] - 1):
        shifted = ext[0, lag : lag + some]
        total = total + jnp.where(ext[1, lag : lag + some] >= lag, taps[lag : lag + 1] * shifted, 0.0)
    out[...] = total.astype(BF16)


def rim_grad(bounds, grad, wse, rim, taps, held):
    rows, channels = grad.shape
    some, width = 2 * RIM, channels // 2
    last = pl.BlockSpec((some, width), lambda i: (rows // some - 1, i))
    wide = lambda height: pl.BlockSpec((height, width), lambda i: (0, i))
    return pl.pallas_call(
        functools.partial(rim_kernel, rows),
        grid=(channels // width,),
        in_specs=[SCALARS, last, last, wide(RIM), wide(taps.shape[0]), pl.BlockSpec(memory_space=pl.ANY)],
        out_specs=last,
        out_shape=jax.ShapeDtypeStruct((rows, channels), BF16),
        scratch_shapes=[pltpu.VMEM((2, some + RIM, width), F32)],
        input_output_aliases={5: 0},
        compiler_params=ROOM,
        cost_estimate=FREE,
    )(bounds, grad, wse, rim, taps, held)


def gate_kernel(bounds, prior, mid, incoming, mirrored, *rest):
    out, mask_own, mask_prior = rest[-3:]
    rows = prior.shape[0]
    earlier, bound, _ = bounds_near(bounds, rows)

    @pl.when(pl.program_id(0) == 0)
    def _():
        mask_own[...] = as_mask(same_tile(grid_of(rows, 0), grid_of(rows, 1), bound), BF16)
        mask_prior[...] = as_mask(tile_before(grid_of(rows, 0), grid_of(rows, 1), bound, earlier, rows), BF16)

    for block in range(prior.shape[1] // LANES):
        at = lanes(block * LANES)

        def matrix_of(group):
            line = block * PER_BLOCK + group
            circle = rolled(mirrored[line : line + 1], rows).astype(BF16)
            return jnp.concatenate([circle * mask_own[...], circle * mask_prior[...]], axis=1)

        pair = jnp.concatenate([mid[:, at], prior[:, at]], axis=0)
        out[:, at] = (incoming[:, at].astype(F32) * filtered(matrix_of, pair, rows)).astype(BF16)


def gate_grad(piece, bounds, prior, mid, incoming, mirrored, held):
    rows, channels = incoming.shape
    part = channels // PIECES
    first = piece * part // BLOCK
    full = lambda: pl.BlockSpec((rows, BLOCK), lambda i: (0, first + i))
    own = lambda: pl.BlockSpec((rows, BLOCK), lambda i: (0, i))
    return pl.pallas_call(
        gate_kernel,
        grid=(part // BLOCK,),
        in_specs=[SCALARS, own(), own(), full(), pl.BlockSpec((BLOCK // GROUP, rows), lambda i: (first + i, 0))]
        + [pl.BlockSpec(memory_space=pl.ANY)] * len(held),
        out_specs=full(),
        out_shape=jax.ShapeDtypeStruct((rows, channels), BF16),
        scratch_shapes=[pltpu.VMEM((rows, rows), BF16)] * 2,
        input_output_aliases={5: 0} if held else {},
        compiler_params=ROOM,
        cost_estimate=FREE,
    )(bounds, prior, mid, incoming, mirrored, *held)


def body(loaded, counts, destinations, bounds, se_gate, mr_gate, phase_grads, se_taps, mr_taps):
    ctx_count = lax.axis_size("ctx")
    rows, channels = loaded.shape[2:]
    group_count = channels // GROUP
    gate_se = se_gate[0]

    incoming = partner(phase_grads[0], "pipe", 1)
    weighted = (mr_gate[0].astype(F32) * incoming.astype(F32)).astype(BF16)
    after = from_behind(weighted, "ctx", -1)
    low, mirrored, taps_se = taps_forms(mr_taps[0], se_taps[0])
    base = own_back(bounds, weighted, incoming, low)

    *outgoing, sent_tail = pick_outgoing(counts, destinations, loaded)
    rim = from_behind(sent_tail, "ctx", 2)
    after, rim, base, low, mirrored, taps_se, *outgoing = lax.optimization_barrier(
        (after, rim, base, low, mirrored, taps_se, *outgoing)
    )
    arrived = [from_behind(piece, "ctx", 1) for piece in outgoing]

    mid_grad, wse = next_back(bounds, after, base, gate_se, low)
    rim_next = from_behind(wse[:RIM], "ctx", -1)
    grad_x = input_grad(bounds, mid_grad, wse, taps_se)
    arrived[0], grad_x = lax.optimization_barrier((arrived[0], grad_x))

    mid, prior, se_sums, gates, lags = [], [], [], (), ()
    for q in range(PIECES):
        mid_piece, gate_piece, se_sum = middle(
            q, bounds, counts, destinations, loaded, arrived[q], rim, gate_se, taps_se, mid_grad, wse, gates
        )
        gates = (gate_piece,)
        lags = (lag_grads(q, bounds, mid_piece, weighted, after, lags),)
        mid.append(mid_piece)
        se_sums.append(se_sum)
        if q < PIECES - 1:
            prior.append(from_behind(mid_piece, "ctx", 1))
    grad_gate_se = gates[0]

    windows = max(group_count // LANES, 1)
    each = PIECES // windows
    se_windows = [sum(se_sums[w * each : (w + 1) * each]) for w in range(windows)]
    total = jnp.concatenate([lags[0], *se_windows], axis=0)
    prior.append(from_behind(mid[-1], "ctx", 1))

    mask = ctx_count // 2
    grad_gate_mr = ()
    while mask > 2:
        total = total + partner(total, "ctx", mask)
        if not grad_gate_mr:
            grad_gate_mr = (gate_grad(0, bounds, prior[0], mid[0], incoming, mirrored, ()),)
            total, *grad_gate_mr = lax.optimization_barrier((total, *grad_gate_mr))
        mask //= 2
    total, rim_next, *prior[1:] = lax.optimization_barrier((total, rim_next, *prior[1:]))
    one, two, three = (partner(total, "ctx", mask) for mask in (1, 2, 3))
    grad_x = rim_grad(bounds, mid_grad, wse, rim_next, taps_se, grad_x)
    for q in range(1, PIECES):
        grad_gate_mr = (gate_grad(q, bounds, prior[q], mid[q], incoming, mirrored, tuple(grad_gate_mr)),)
    total = (total + one) + (two + three)

    scale = 1.0 / math.sqrt(ctx_count * rows * GROUP)
    total = total * scale
    mr_total = total[:group_count]
    se_total = total[group_count:].reshape(windows, RIM, -1).transpose(0, 2, 1)
    se_total = se_total.reshape(group_count, RIM)[:, : se_taps.shape[2]]
    return (grad_x[None], grad_gate_se[None], grad_gate_mr[0][None], se_total[None], mr_total[None])


def solution(mesh):
    return jax.shard_map(
        body,
        mesh=mesh,
        in_specs=(
            P("pipe", "ctx", None, None),
            P("ctx"),
            P("ctx"),
            P(),
            P("pipe", "ctx", None),
            P("pipe", "ctx", None),
            P("pipe", "ctx", None),
            P("pipe", None, None),
            P("pipe", None, None),
        ),
        out_specs=(
            P("pipe", "ctx", None),
            P("pipe", "ctx", None),
            P("pipe", "ctx", None),
            P("pipe", None, None),
            P("pipe", None, None),
        ),
        check_vma=False,
    )
```

```python
import functools
import math

import jax
import jax.numpy as jnp
from jax import lax
from jax.experimental import pallas as pl
from jax.experimental.pallas import tpu as pltpu
from jax.sharding import PartitionSpec as P

GROUP = 16
LANES = 128
PER_BLOCK = LANES // GROUP
RIM = 8
FAR = 1 << 20
PIECES = 2
BLOCK = 2048

F32 = jnp.float32
BF16 = jnp.bfloat16


def from_behind(block, axis, distance):
    devices = range(lax.axis_size(axis))
    route = [(i - distance, i) for i in devices if i - distance in devices]
    return lax.ppermute(block, axis, route)


def partner(value, axis, mask):
    pairs = [(source, source ^ mask) for source in range(lax.axis_size(axis))]
    return lax.ppermute(value, axis, pairs)


def exchange_order(count):
    masks = [1 << bit for bit in range(count.bit_length() - 1)]
    return masks[1:] + masks[:1]


def grid_of(rows, which):
    return lax.broadcasted_iota(jnp.int32, (rows, rows), which)


def same_tile(out_row, in_row, bound):
    return (out_row >= in_row) & ((out_row < bound) | (in_row >= bound))


def tile_before(out_row, in_row, bound, earlier, rows):
    return (out_row < in_row) & (out_row < bound) & ((earlier >= rows) | (in_row >= earlier))


def as_mask(flags, dtype):
    return jnp.where(flags, 1.0, 0.0).astype(F32).astype(dtype)


def room_of(row, bound, earlier, rows):
    before = jnp.where(earlier < rows, row + (rows - earlier), FAR)
    return jnp.where(row >= bound, row - bound, before)


def rolled(line, rows):
    return pltpu.roll(jnp.broadcast_to(line, (rows, rows)), 0, 1, stride=1, stride_axis=0)


def lanes(start):
    return pl.ds(start, LANES)


def bounds_near(bounds, rows):
    count = bounds.shape[0]
    shard = lax.axis_index("ctx")
    near = []
    for tile in (shard - 1, shard, shard + 1):
        bound = bounds[jnp.clip(tile, 0, count - 1)]
        near.append(jnp.where((tile >= 0) & (tile < count), bound, rows))
    return near


def holds_own(counts, destinations):
    return (counts[0] >= 1) & (destinations[0] == lax.axis_index("ctx"))


SCALARS = pl.BlockSpec(memory_space=pltpu.SMEM)
FREE = pl.CostEstimate(flops=1, bytes_accessed=1, transcendentals=0)
ROOM = pltpu.CompilerParams(vmem_limit_bytes=40 << 20)


def pick_kernel(counts, destinations, slot, first, *outs):
    *pieces, sent_tail = outs
    rows = slot.shape[0]
    shard = lax.axis_index("ctx")
    sends = ((counts[0] >= 1) & (destinations[0] == shard + 1)) | ((counts[0] >= 2) & (destinations[1] == shard + 1))
    picked = slot[...]
    own = jnp.where(holds_own(counts, destinations), first[...].astype(F32), 0.0)[-RIM:].astype(BF16)
    for number, piece in enumerate(pieces):

        @pl.when(pl.program_id(0) == number)
        def _(piece=piece):
            piece[:rows] = picked
            piece[rows:] = own

    sent_tail[...] = jnp.where(sends, picked[-2 * RIM :].astype(F32), 0.0)[-RIM:].astype(BF16)


def pick_outgoing(counts, destinations, loaded):
    rows, channels = loaded.shape[2:]
    width = channels // PIECES
    shape = lambda height, size: jax.ShapeDtypeStruct((height, size), loaded.dtype)
    return pl.pallas_call(
        pick_kernel,
        grid_spec=pltpu.PrefetchScalarGridSpec(
            num_scalar_prefetch=2,
            grid=(PIECES,),
            in_specs=[
                pl.BlockSpec((None, None, rows, width), lambda i, held, _: (0, jnp.where(held[0] == 2, 1, 0), 0, i)),
                pl.BlockSpec((None, None, 2 * RIM, width), lambda i, *_: (0, 0, rows // (2 * RIM) - 1, i)),
            ],
            out_specs=[pl.BlockSpec((rows + RIM, width), lambda i, *_: (0, 0))] * PIECES
            + [pl.BlockSpec((RIM, width), lambda i, *_: (0, i))],
        ),
        out_shape=[shape(rows + RIM, width)] * PIECES + [shape(RIM, channels)],
        cost_estimate=FREE,
    )(counts, destinations, loaded, loaded)


def taps_kernel(mr, se, low, mirrored, spread):
    groups, count = mr.shape
    rounded = mr[...].astype(BF16)
    low[...] = rounded.astype(F32)
    mirror = as_mask(lax.rem(grid_of(count, 0) + grid_of(count, 1), count) == 0, BF16)
    mirrored[...] = jnp.dot(rounded, mirror, preferred_element_type=F32)
    taps = se.shape[1]
    group = lax.broadcasted_iota(jnp.int32, (PER_BLOCK, LANES), 0)
    owner = lax.broadcasted_iota(jnp.int32, (PER_BLOCK, LANES), 1) // GROUP
    widen = as_mask(group == owner, F32)
    for block in range(groups // PER_BLOCK):
        part = se[block * PER_BLOCK : (block + 1) * PER_BLOCK]
        for tap in range(taps):
            line = jnp.sum(part[:, tap : tap + 1] * widen, axis=0, keepdims=True)
            spread[tap : tap + 1, lanes(block * LANES)] = line
    spread[taps:] = jnp.zeros((spread.shape[0] - taps, spread.shape[1]), F32)


def taps_forms(mr_taps, se_taps):
    groups, count = mr_taps.shape
    return pl.pallas_call(
        taps_kernel,
        out_shape=[
            jax.ShapeDtypeStruct((groups, count), F32),
            jax.ShapeDtypeStruct((groups, count), F32),
            jax.ShapeDtypeStruct((RIM, groups * GROUP), F32),
        ],
        cost_estimate=FREE,
    )(mr_taps, se_taps)


def filtered(matrix_of, values, rows):
    lane_group = lax.broadcasted_iota(jnp.int32, (rows, LANES), 1) // GROUP
    total = jnp.zeros((rows, LANES), F32)
    for group in range(PER_BLOCK):
        product = jnp.dot(matrix_of(group), values, preferred_element_type=F32)
        total = jnp.where(lane_group == group, product, total)
    return total


def own_back_kernel(bounds, weighted, incoming, low, out, mask):
    rows = weighted.shape[0]
    _, bound, _ = bounds_near(bounds, rows)

    @pl.when(pl.program_id(0) == 0)
    def _():
        mask[...] = as_mask(same_tile(grid_of(rows, 1), grid_of(rows, 0), bound), BF16)

    for block in range(weighted.shape[1] // LANES):
        at = lanes(block * LANES)

        def matrix_of(group):
            line = block * PER_BLOCK + group
            return rolled(low[line : line + 1], rows).astype(BF16) * mask[...]

        out[:, at] = incoming[:, at].astype(F32) + filtered(matrix_of, weighted[:, at], rows)


def own_back(bounds, weighted, incoming, low):
    rows, channels = weighted.shape
    wide = lambda height: pl.BlockSpec((height, BLOCK), lambda i: (0, i))
    return pl.pallas_call(
        own_back_kernel,
        grid=(channels // BLOCK,),
        in_specs=[SCALARS, wide(rows), wide(rows), pl.BlockSpec((BLOCK // GROUP, rows), lambda i: (i, 0))],
        out_specs=wide(rows),
        out_shape=jax.ShapeDtypeStruct((rows, channels), F32),
        scratch_shapes=[pltpu.VMEM((rows, rows), BF16)],
        compiler_params=ROOM,
        cost_estimate=FREE,
    )(bounds, weighted, incoming, low)


def next_back_kernel(bounds, after, base, gate, low, mid_grad, wse, mask):
    rows = after.shape[0]
    _, bound, later = bounds_near(bounds, rows)

    @pl.when(pl.program_id(0) == 0)
    def _():
        mask[...] = as_mask(tile_before(grid_of(rows, 1), grid_of(rows, 0), later, bound, rows), BF16)

    for block in range(after.shape[1] // LANES):
        at = lanes(block * LANES)

        def matrix_of(group):
            line = block * PER_BLOCK + group
            return rolled(low[line : line + 1], rows).astype(BF16) * mask[...]

        grad = (base[:, at] + filtered(matrix_of, after[:, at], rows)).astype(BF16)
        mid_grad[:, at] = grad
        wse[:, at] = (gate[:, at].astype(F32) * grad.astype(F32)).astype(BF16)


def next_back(bounds, after, base, gate, low):
    rows, channels = after.shape
    wide = lambda height: pl.BlockSpec((height, BLOCK), lambda i: (0, i))
    return pl.pallas_call(
        next_back_kernel,
        grid=(channels // BLOCK,),
        in_specs=[
            SCALARS,
            wide(rows),
            wide(rows),
            wide(rows),
            pl.BlockSpec((BLOCK // GROUP, rows), lambda i: (i, 0)),
        ],
        out_specs=[wide(rows)] * 2,
        out_shape=[jax.ShapeDtypeStruct((rows, channels), BF16)] * 2,
        scratch_shapes=[pltpu.VMEM((rows, rows), BF16)],
        compiler_params=ROOM,
        cost_estimate=FREE,
    )(bounds, after, base, gate, low)


def middle_kernel(shift, bounds, counts, destinations, slot, arrived, rim, gate, taps, grad, wse, *rest):
    mid_out, gate_grad, se_out, ext, room, spread = rest[-6:]
    rows = slot.shape[0]
    step = pl.program_id(0)
    earlier, bound, _ = bounds_near(bounds, rows)
    own_here = holds_own(counts, destinations)

    @pl.when(step == 0)
    def _():
        row = lax.broadcasted_iota(jnp.int32, (rows, LANES), 0)
        room[...] = room_of(row, bound, earlier, rows)
        se_out[...] = jnp.zeros_like(se_out)
        spread[...] = as_mask(grid_of(LANES, 0) // GROUP == grid_of(LANES, 1), BF16)

    blocks = slot.shape[1] // LANES
    thirds = []
    for block in range(blocks):
        at = lanes(block * LANES)
        x = jnp.where(own_here, slot[:, at].astype(F32), arrived[:rows, at].astype(F32))
        ext[block, :RIM] = arrived[rows:, at].astype(F32) + rim[:, at].astype(F32)
        ext[block, RIM:] = x
        mix = jnp.zeros((rows, LANES), F32)
        wide_wse = wse[:, at].astype(F32)
        sums = []
        for lag in range(taps.shape[0] - 1):
            kept = jnp.where(room[...] >= lag, ext[block, RIM - lag : RIM - lag + rows], 0.0)
            mix = mix + taps[lag : lag + 1, at] * kept
            sums.append(jnp.sum(wide_wse * kept, axis=0, keepdims=True))
        sums.append(jnp.zeros((1, LANES), F32))
        mid_out[:, at] = (x + gate[:, at].astype(F32) * mix).astype(BF16)
        gate_grad[:, at] = (grad[:, at].astype(F32) * mix).astype(BF16)
        left = jnp.concatenate(sums, axis=0)
        for _ in range(3):
            term = left.astype(BF16).astype(F32)
            thirds.append(term)
            left = left - term
    parts = jnp.dot(jnp.concatenate(thirds, axis=0).astype(BF16), spread[...], preferred_element_type=F32)
    gathered = jnp.zeros((RIM, LANES), F32)
    for block in range(blocks):
        first = 3 * RIM * block
        part = parts[first : first + RIM] + parts[first + RIM : first + 2 * RIM] + parts[first + 2 * RIM : first + 3 * RIM]
        gathered = gathered + (pltpu.roll(part, block * PER_BLOCK, 1) if block else part)
    place = lax.rem(shift + step * blocks * PER_BLOCK, LANES)
    se_out[...] += pltpu.roll(gathered, place, 1)


def middle(piece, bounds, counts, destinations, loaded, arrived, rim, gate, taps, grad, wse, held):
    rows, channels = gate.shape
    part = channels // PIECES
    groups = channels // GROUP
    first = piece * part // BLOCK
    full = lambda height: pl.BlockSpec((height, BLOCK), lambda i: (0, first + i))
    own = lambda height: pl.BlockSpec((height, BLOCK), lambda i: (0, i))
    return pl.pallas_call(
        functools.partial(middle_kernel, (piece * groups // PIECES) % LANES),
        grid=(part // BLOCK,),
        in_specs=[
            SCALARS,
            SCALARS,
            SCALARS,
            pl.BlockSpec((None, None, rows, BLOCK), lambda i: (0, 0, 0, first + i)),
            own(rows + RIM),
            full(RIM),
            full(rows),
            full(taps.shape[0]),
            full(rows),
            full(rows),
        ]
        + [pl.BlockSpec(memory_space=pl.ANY)] * len(held),
        out_specs=[own(rows), full(rows), pl.BlockSpec((RIM, LANES), lambda i: (0, 0))],
        out_shape=[
            jax.ShapeDtypeStruct((rows, part), BF16),
            jax.ShapeDtypeStruct((rows, channels), BF16),
            jax.ShapeDtypeStruct((RIM, LANES), F32),
        ],
        scratch_shapes=[
            pltpu.VMEM((BLOCK // LANES, rows + RIM, LANES), F32),
            pltpu.VMEM((rows, LANES), jnp.int32),
            pltpu.VMEM((LANES, LANES), BF16),
        ],
        input_output_aliases={10: 1} if held else {},
        compiler_params=ROOM,
        cost_estimate=FREE,
    )(bounds, counts, destinations, loaded, arrived, rim, gate, taps, grad, wse, *held)


def lag_kernel(bounds, mid, weighted, after, *rest):
    out, lag_own, lag_next, flip, flipped = rest[-5:]
    rows = mid.shape[0]
    _, bound, later = bounds_near(bounds, rows)

    @pl.when(pl.program_id(0) == 0)
    def _():
        target = grid_of(rows, 1)
        mirrored = rows - 1 - grid_of(rows, 0)
        lag_own[...] = as_mask(same_tile(target, mirrored, bound), F32)
        lag_next[...] = as_mask(tile_before(target, mirrored, later, bound, rows), F32)
        flip[...] = as_mask(mirrored == target, BF16)

    one_row = lax.broadcasted_iota(jnp.int32, (1, LANES), 1) // GROUP
    for block in range(mid.shape[1] // LANES):
        flipped[block] = jnp.dot(flip[...], mid[:, lanes(block * LANES)], preferred_element_type=F32).astype(BF16)
    for block in range(mid.shape[1] // LANES):
        at = lanes(block * LANES)
        pair = jnp.concatenate([weighted[:, at], after[:, at]], axis=0).T
        mirrored_mid = flipped[block]
        lags = []
        for group in range(PER_BLOCK):
            chosen = mirrored_mid * as_mask(one_row == group, BF16)
            products = jnp.dot(chosen, pair, preferred_element_type=F32)
            kept = products[:, :rows] * lag_own[...] + products[:, rows:] * lag_next[...]
            kept = pltpu.roll(kept, 1, 1, stride=1, stride_axis=0)
            lags.append(jnp.sum(kept, axis=0, keepdims=True))
        out[block * PER_BLOCK : (block + 1) * PER_BLOCK] = jnp.concatenate(lags, axis=0)


def lag_grads(piece, bounds, mid, weighted, after, held):
    rows, channels = weighted.shape
    part = channels // PIECES
    first = piece * part // BLOCK
    full = lambda height: pl.BlockSpec((height, BLOCK), lambda i: (0, first + i))
    square = lambda dtype: pltpu.VMEM((rows, rows), dtype)
    return pl.pallas_call(
        lag_kernel,
        grid=(part // BLOCK,),
        in_specs=[SCALARS, pl.BlockSpec((rows, BLOCK), lambda i: (0, i)), full(rows), full(rows)]
        + [pl.BlockSpec(memory_space=pl.ANY)] * len(held),
        out_specs=pl.BlockSpec((BLOCK // GROUP, rows), lambda i: (first + i, 0)),
        out_shape=jax.ShapeDtypeStruct((channels // GROUP, rows), F32),
        scratch_shapes=[square(F32), square(F32), square(BF16), pltpu.VMEM((BLOCK // LANES, rows, LANES), BF16)],
        input_output_aliases={4: 0} if held else {},
        compiler_params=ROOM,
        cost_estimate=FREE,
    )(bounds, mid, weighted, after, *held)


def input_kernel(bounds, grad, wse, taps, out, ext, room):
    rows = out.shape[0]
    earlier, bound, _ = bounds_near(bounds, rows)

    @pl.when(pl.program_id(0) == 0)
    def _():
        row = lax.broadcasted_iota(jnp.int32, (rows, LANES), 0)
        room[:rows] = room_of(row, bound, earlier, rows)
        room[rows:] = jnp.zeros((RIM, LANES), jnp.int32)

    for block in range(out.shape[1] // LANES):
        at = lanes(block * LANES)
        ext[block, :rows] = wse[:, at].astype(F32)
        ext[block, rows:] = jnp.zeros((RIM, LANES), F32)
        total = grad[:, at].astype(F32)
        for lag in range(taps.shape[0] - 1):
            shifted = ext[block, lag : lag + rows]
            total = total + jnp.where(room[lag : lag + rows] >= lag, taps[lag : lag + 1, at] * shifted, 0.0)
        out[:, at] = total.astype(BF16)


def input_grad(bounds, grad, wse, taps):
    rows, channels = grad.shape
    wide = lambda height: pl.BlockSpec((height, BLOCK), lambda i: (0, i))
    return pl.pallas_call(
        input_kernel,
        grid=(channels // BLOCK,),
        in_specs=[SCALARS, wide(rows), wide(rows), wide(taps.shape[0])],
        out_specs=wide(rows),
        out_shape=jax.ShapeDtypeStruct((rows, channels), BF16),
        scratch_shapes=[
            pltpu.VMEM((BLOCK // LANES, rows + RIM, LANES), F32),
            pltpu.VMEM((rows + RIM, LANES), jnp.int32),
        ],
        compiler_params=ROOM,
        cost_estimate=FREE,
    )(bounds, grad, wse, taps)


def rim_kernel(rows, bounds, grad, wse, rim, taps, held, out, ext):
    del held
    some = out.shape[0]
    earlier, bound, later = bounds_near(bounds, rows)
    row = lax.broadcasted_iota(jnp.int32, (some, out.shape[1]), 0) + (rows - some)
    rim_row = lax.broadcasted_iota(jnp.int32, (RIM, out.shape[1]), 0)
    ext[0, :some] = wse[...].astype(F32)
    ext[0, some:] = rim[...].astype(F32)
    ext[1, :some] = room_of(row, bound, earlier, rows).astype(F32)
    ext[1, some:] = room_of(rim_row, later, bound, rows).astype(F32)
    total = grad[...].astype(F32)
    for lag in range(taps.shape[0] - 1):
        shifted = ext[0, lag : lag + some]
        total = total + jnp.where(ext[1, lag : lag + some] >= lag, taps[lag : lag + 1] * shifted, 0.0)
    out[...] = total.astype(BF16)


def rim_grad(bounds, grad, wse, rim, taps, held):
    rows, channels = grad.shape
    some, width = 2 * RIM, channels // 2
    last = pl.BlockSpec((some, width), lambda i: (rows // some - 1, i))
    wide = lambda height: pl.BlockSpec((height, width), lambda i: (0, i))
    return pl.pallas_call(
        functools.partial(rim_kernel, rows),
        grid=(channels // width,),
        in_specs=[SCALARS, last, last, wide(RIM), wide(taps.shape[0]), pl.BlockSpec(memory_space=pl.ANY)],
        out_specs=last,
        out_shape=jax.ShapeDtypeStruct((rows, channels), BF16),
        scratch_shapes=[pltpu.VMEM((2, some + RIM, width), F32)],
        input_output_aliases={5: 0},
        compiler_params=ROOM,
        cost_estimate=FREE,
    )(bounds, grad, wse, rim, taps, held)


def gate_kernel(bounds, prior, mid, incoming, mirrored, *rest):
    out, mask_own, mask_prior = rest[-3:]
    rows = prior.shape[0]
    earlier, bound, _ = bounds_near(bounds, rows)

    @pl.when(pl.program_id(0) == 0)
    def _():
        mask_own[...] = as_mask(same_tile(grid_of(rows, 0), grid_of(rows, 1), bound), BF16)
        mask_prior[...] = as_mask(tile_before(grid_of(rows, 0), grid_of(rows, 1), bound, earlier, rows), BF16)

    for block in range(prior.shape[1] // LANES):
        at = lanes(block * LANES)

        def matrix_of(group):
            line = block * PER_BLOCK + group
            circle = rolled(mirrored[line : line + 1], rows).astype(BF16)
            return jnp.concatenate([circle * mask_own[...], circle * mask_prior[...]], axis=1)

        pair = jnp.concatenate([mid[:, at], prior[:, at]], axis=0)
        out[:, at] = (incoming[:, at].astype(F32) * filtered(matrix_of, pair, rows)).astype(BF16)


def gate_grad(piece, bounds, prior, mid, incoming, mirrored, held):
    rows, channels = incoming.shape
    part = channels // PIECES
    first = piece * part // BLOCK
    full = lambda: pl.BlockSpec((rows, BLOCK), lambda i: (0, first + i))
    own = lambda: pl.BlockSpec((rows, BLOCK), lambda i: (0, i))
    return pl.pallas_call(
        gate_kernel,
        grid=(part // BLOCK,),
        in_specs=[SCALARS, own(), own(), full(), pl.BlockSpec((BLOCK // GROUP, rows), lambda i: (first + i, 0))]
        + [pl.BlockSpec(memory_space=pl.ANY)] * len(held),
        out_specs=full(),
        out_shape=jax.ShapeDtypeStruct((rows, channels), BF16),
        scratch_shapes=[pltpu.VMEM((rows, rows), BF16)] * 2,
        input_output_aliases={5: 0} if held else {},
        compiler_params=ROOM,
        cost_estimate=FREE,
    )(bounds, prior, mid, incoming, mirrored, *held)


def body(loaded, counts, destinations, bounds, se_gate, mr_gate, phase_grads, se_taps, mr_taps):
    ctx_count = lax.axis_size("ctx")
    rows, channels = loaded.shape[2:]
    group_count = channels // GROUP
    gate_se = se_gate[0]

    incoming = partner(phase_grads[0], "pipe", 1)
    weighted = (mr_gate[0].astype(F32) * incoming.astype(F32)).astype(BF16)
    after = from_behind(weighted, "ctx", -1)
    low, mirrored, taps_se = taps_forms(mr_taps[0], se_taps[0])
    base = own_back(bounds, weighted, incoming, low)

    *outgoing, sent_tail = pick_outgoing(counts, destinations, loaded)
    rim = from_behind(sent_tail, "ctx", 2)
    after, rim, base, low, mirrored, taps_se, *outgoing = lax.optimization_barrier(
        (after, rim, base, low, mirrored, taps_se, *outgoing)
    )
    arrived = [from_behind(piece, "ctx", 1) for piece in outgoing]

    mid_grad, wse = next_back(bounds, after, base, gate_se, low)
    grad_x = input_grad(bounds, mid_grad, wse, taps_se)
    arrived[0], grad_x = lax.optimization_barrier((arrived[0], grad_x))

    mid, prior, se_sums, gates, lags = [], [], [], (), ()
    for q in range(PIECES):
        mid_piece, gate_piece, se_sum = middle(
            q, bounds, counts, destinations, loaded, arrived[q], rim, gate_se, taps_se, mid_grad, wse, gates
        )
        gates = (gate_piece,)
        lags = (lag_grads(q, bounds, mid_piece, weighted, after, lags),)
        mid.append(mid_piece)
        se_sums.append(se_sum)
        if q < PIECES - 1:
            prior.append(from_behind(mid_piece, "ctx", 1))
    grad_gate_se = gates[0]

    windows = max(group_count // LANES, 1)
    each = PIECES // windows
    se_windows = [sum(se_sums[w * each : (w + 1) * each]) for w in range(windows)]
    total = jnp.concatenate([lags[0], *se_windows], axis=0)
    total, mid[-1] = lax.optimization_barrier((total, mid[-1]))
    prior.append(from_behind(mid[-1], "ctx", 1))
    grad_gate_mr = (gate_grad(0, bounds, prior[0], mid[0], incoming, mirrored, ()),)
    total, wse, *grad_gate_mr = lax.optimization_barrier((total, wse, *grad_gate_mr))
    rim_next = from_behind(wse[:RIM], "ctx", -1)

    mask = ctx_count // 2
    while mask > 2:
        total = total + partner(total, "ctx", mask)
        if mask == 4:
            for q in range(1, PIECES):
                grad_gate_mr = (gate_grad(q, bounds, prior[q], mid[q], incoming, mirrored, tuple(grad_gate_mr)),)
            total, *grad_gate_mr = lax.optimization_barrier((total, *grad_gate_mr))
        else:
            total, rim_next = lax.optimization_barrier((total, rim_next))
        mask //= 2
    one, two, three = (partner(total, "ctx", mask) for mask in (1, 2, 3))
    grad_x = rim_grad(bounds, mid_grad, wse, rim_next, taps_se, grad_x)
    total = (total + one) + (two + three)

    scale = 1.0 / math.sqrt(ctx_count * rows * GROUP)
    total = total * scale
    mr_total = total[:group_count]
    se_total = total[group_count:].reshape(windows, RIM, -1).transpose(0, 2, 1)
    se_total = se_total.reshape(group_count, RIM)[:, : se_taps.shape[2]]
    return (grad_x[None], grad_gate_se[None], grad_gate_mr[0][None], se_total[None], mr_total[None])


def solution(mesh):
    return jax.shard_map(
        body,
        mesh=mesh,
        in_specs=(
            P("pipe", "ctx", None, None),
            P("ctx"),
            P("ctx"),
            P(),
            P("pipe", "ctx", None),
            P("pipe", "ctx", None),
            P("pipe", "ctx", None),
            P("pipe", None, None),
            P("pipe", None, None),
        ),
        out_specs=(
            P("pipe", "ctx", None),
            P("pipe", "ctx", None),
            P("pipe", "ctx", None),
            P("pipe", None, None),
            P("pipe", None, None),
        ),
        check_vma=False,
    )
```

```python
import functools
import math

import jax
import jax.numpy as jnp
from jax import lax
from jax.experimental import pallas as pl
from jax.experimental.pallas import tpu as pltpu
from jax.sharding import PartitionSpec as P

GROUP = 16
LANES = 128
PER_BLOCK = LANES // GROUP
RIM = 8
FAR = 1 << 20
PIECES = 2
BLOCK = 2048

F32 = jnp.float32
BF16 = jnp.bfloat16


def from_behind(block, axis, distance):
    devices = range(lax.axis_size(axis))
    route = [(i - distance, i) for i in devices if i - distance in devices]
    return lax.ppermute(block, axis, route)


def partner(value, axis, mask):
    pairs = [(source, source ^ mask) for source in range(lax.axis_size(axis))]
    return lax.ppermute(value, axis, pairs)


def exchange_order(count):
    masks = [1 << bit for bit in range(count.bit_length() - 1)]
    return masks[1:] + masks[:1]


def grid_of(rows, which):
    return lax.broadcasted_iota(jnp.int32, (rows, rows), which)


def same_tile(out_row, in_row, bound):
    return (out_row >= in_row) & ((out_row < bound) | (in_row >= bound))


def tile_before(out_row, in_row, bound, earlier, rows):
    return (out_row < in_row) & (out_row < bound) & ((earlier >= rows) | (in_row >= earlier))


def as_mask(flags, dtype):
    return jnp.where(flags, 1.0, 0.0).astype(F32).astype(dtype)


def room_of(row, bound, earlier, rows):
    before = jnp.where(earlier < rows, row + (rows - earlier), FAR)
    return jnp.where(row >= bound, row - bound, before)


def rolled(line, rows):
    return pltpu.roll(jnp.broadcast_to(line, (rows, rows)), 0, 1, stride=1, stride_axis=0)


def lanes(start):
    return pl.ds(start, LANES)


def bounds_near(bounds, rows):
    count = bounds.shape[0]
    shard = lax.axis_index("ctx")
    near = []
    for tile in (shard - 1, shard, shard + 1):
        bound = bounds[jnp.clip(tile, 0, count - 1)]
        near.append(jnp.where((tile >= 0) & (tile < count), bound, rows))
    return near


def holds_own(counts, destinations):
    return (counts[0] >= 1) & (destinations[0] == lax.axis_index("ctx"))


SCALARS = pl.BlockSpec(memory_space=pltpu.SMEM)
FREE = pl.CostEstimate(flops=1, bytes_accessed=1, transcendentals=0)
ROOM = pltpu.CompilerParams(vmem_limit_bytes=40 << 20)


def pick_kernel(counts, destinations, slot, first, *outs):
    *pieces, sent_tail = outs
    rows = slot.shape[0]
    shard = lax.axis_index("ctx")
    sends = ((counts[0] >= 1) & (destinations[0] == shard + 1)) | ((counts[0] >= 2) & (destinations[1] == shard + 1))
    picked = slot[...]
    own = jnp.where(holds_own(counts, destinations), first[...].astype(F32), 0.0)[-RIM:].astype(BF16)
    for number, piece in enumerate(pieces):

        @pl.when(pl.program_id(0) == number)
        def _(piece=piece):
            piece[:rows] = picked
            piece[rows:] = own

    sent_tail[...] = jnp.where(sends, picked[-2 * RIM :].astype(F32), 0.0)[-RIM:].astype(BF16)


def pick_outgoing(counts, destinations, loaded):
    rows, channels = loaded.shape[2:]
    width = channels // PIECES
    shape = lambda height, size: jax.ShapeDtypeStruct((height, size), loaded.dtype)
    return pl.pallas_call(
        pick_kernel,
        grid_spec=pltpu.PrefetchScalarGridSpec(
            num_scalar_prefetch=2,
            grid=(PIECES,),
            in_specs=[
                pl.BlockSpec((None, None, rows, width), lambda i, held, _: (0, jnp.where(held[0] == 2, 1, 0), 0, i)),
                pl.BlockSpec((None, None, 2 * RIM, width), lambda i, *_: (0, 0, rows // (2 * RIM) - 1, i)),
            ],
            out_specs=[pl.BlockSpec((rows + RIM, width), lambda i, *_: (0, 0))] * PIECES
            + [pl.BlockSpec((RIM, width), lambda i, *_: (0, i))],
        ),
        out_shape=[shape(rows + RIM, width)] * PIECES + [shape(RIM, channels)],
        cost_estimate=FREE,
    )(counts, destinations, loaded, loaded)


def taps_kernel(mr, se, low, mirrored, spread):
    groups, count = mr.shape
    rounded = mr[...].astype(BF16)
    low[...] = rounded.astype(F32)
    mirror = as_mask(lax.rem(grid_of(count, 0) + grid_of(count, 1), count) == 0, BF16)
    mirrored[...] = jnp.dot(rounded, mirror, preferred_element_type=F32)
    taps = se.shape[1]
    group = lax.broadcasted_iota(jnp.int32, (PER_BLOCK, LANES), 0)
    owner = lax.broadcasted_iota(jnp.int32, (PER_BLOCK, LANES), 1) // GROUP
    widen = as_mask(group == owner, F32)
    for block in range(groups // PER_BLOCK):
        part = se[block * PER_BLOCK : (block + 1) * PER_BLOCK]
        for tap in range(taps):
            line = jnp.sum(part[:, tap : tap + 1] * widen, axis=0, keepdims=True)
            spread[tap : tap + 1, lanes(block * LANES)] = line
    spread[taps:] = jnp.zeros((spread.shape[0] - taps, spread.shape[1]), F32)


def taps_forms(mr_taps, se_taps):
    groups, count = mr_taps.shape
    return pl.pallas_call(
        taps_kernel,
        out_shape=[
            jax.ShapeDtypeStruct((groups, count), F32),
            jax.ShapeDtypeStruct((groups, count), F32),
            jax.ShapeDtypeStruct((RIM, groups * GROUP), F32),
        ],
        cost_estimate=FREE,
    )(mr_taps, se_taps)


def filtered(matrix_of, values, rows):
    lane_group = lax.broadcasted_iota(jnp.int32, (rows, LANES), 1) // GROUP
    total = jnp.zeros((rows, LANES), F32)
    for group in range(PER_BLOCK):
        product = jnp.dot(matrix_of(group), values, preferred_element_type=F32)
        total = jnp.where(lane_group == group, product, total)
    return total


def own_back_kernel(bounds, weighted, incoming, low, out, mask):
    rows = weighted.shape[0]
    _, bound, _ = bounds_near(bounds, rows)

    @pl.when(pl.program_id(0) == 0)
    def _():
        mask[...] = as_mask(same_tile(grid_of(rows, 1), grid_of(rows, 0), bound), BF16)

    for block in range(weighted.shape[1] // LANES):
        at = lanes(block * LANES)

        def matrix_of(group):
            line = block * PER_BLOCK + group
            return rolled(low[line : line + 1], rows).astype(BF16) * mask[...]

        out[:, at] = incoming[:, at].astype(F32) + filtered(matrix_of, weighted[:, at], rows)


def own_back(bounds, weighted, incoming, low):
    rows, channels = weighted.shape
    wide = lambda height: pl.BlockSpec((height, BLOCK), lambda i: (0, i))
    return pl.pallas_call(
        own_back_kernel,
        grid=(channels // BLOCK,),
        in_specs=[SCALARS, wide(rows), wide(rows), pl.BlockSpec((BLOCK // GROUP, rows), lambda i: (i, 0))],
        out_specs=wide(rows),
        out_shape=jax.ShapeDtypeStruct((rows, channels), F32),
        scratch_shapes=[pltpu.VMEM((rows, rows), BF16)],
        compiler_params=ROOM,
        cost_estimate=FREE,
    )(bounds, weighted, incoming, low)


def next_back_kernel(bounds, after, base, gate, low, mid_grad, wse, mask):
    rows = after.shape[0]
    _, bound, later = bounds_near(bounds, rows)

    @pl.when(pl.program_id(0) == 0)
    def _():
        mask[...] = as_mask(tile_before(grid_of(rows, 1), grid_of(rows, 0), later, bound, rows), BF16)

    for block in range(after.shape[1] // LANES):
        at = lanes(block * LANES)

        def matrix_of(group):
            line = block * PER_BLOCK + group
            return rolled(low[line : line + 1], rows).astype(BF16) * mask[...]

        grad = (base[:, at] + filtered(matrix_of, after[:, at], rows)).astype(BF16)
        mid_grad[:, at] = grad
        wse[:, at] = (gate[:, at].astype(F32) * grad.astype(F32)).astype(BF16)


def next_back(bounds, after, base, gate, low):
    rows, channels = after.shape
    wide = lambda height: pl.BlockSpec((height, BLOCK), lambda i: (0, i))
    return pl.pallas_call(
        next_back_kernel,
        grid=(channels // BLOCK,),
        in_specs=[
            SCALARS,
            wide(rows),
            wide(rows),
            wide(rows),
            pl.BlockSpec((BLOCK // GROUP, rows), lambda i: (i, 0)),
        ],
        out_specs=[wide(rows)] * 2,
        out_shape=[jax.ShapeDtypeStruct((rows, channels), BF16)] * 2,
        scratch_shapes=[pltpu.VMEM((rows, rows), BF16)],
        compiler_params=ROOM,
        cost_estimate=FREE,
    )(bounds, after, base, gate, low)


def middle_kernel(shift, bounds, counts, destinations, slot, arrived, rim, gate, taps, grad, wse, *rest):
    mid_out, gate_grad, se_out, ext, room, spread = rest[-6:]
    rows = slot.shape[0]
    step = pl.program_id(0)
    earlier, bound, _ = bounds_near(bounds, rows)
    own_here = holds_own(counts, destinations)

    @pl.when(step == 0)
    def _():
        row = lax.broadcasted_iota(jnp.int32, (rows, LANES), 0)
        room[...] = room_of(row, bound, earlier, rows)
        se_out[...] = jnp.zeros_like(se_out)
        spread[...] = as_mask(grid_of(LANES, 0) // GROUP == grid_of(LANES, 1), BF16)

    blocks = slot.shape[1] // LANES
    thirds = []
    for block in range(blocks):
        at = lanes(block * LANES)
        x = jnp.where(own_here, slot[:, at].astype(F32), arrived[:rows, at].astype(F32))
        ext[block, :RIM] = arrived[rows:, at].astype(F32) + rim[:, at].astype(F32)
        ext[block, RIM:] = x
        mix = jnp.zeros((rows, LANES), F32)
        wide_wse = wse[:, at].astype(F32)
        sums = []
        for lag in range(taps.shape[0] - 1):
            kept = jnp.where(room[...] >= lag, ext[block, RIM - lag : RIM - lag + rows], 0.0)
            mix = mix + taps[lag : lag + 1, at] * kept
            sums.append(jnp.sum(wide_wse * kept, axis=0, keepdims=True))
        sums.append(jnp.zeros((1, LANES), F32))
        mid_out[:, at] = (x + gate[:, at].astype(F32) * mix).astype(BF16)
        gate_grad[:, at] = (grad[:, at].astype(F32) * mix).astype(BF16)
        left = jnp.concatenate(sums, axis=0)
        for _ in range(3):
            term = left.astype(BF16).astype(F32)
            thirds.append(term)
            left = left - term
    parts = jnp.dot(jnp.concatenate(thirds, axis=0).astype(BF16), spread[...], preferred_element_type=F32)
    gathered = jnp.zeros((RIM, LANES), F32)
    for block in range(blocks):
        first = 3 * RIM * block
        part = parts[first : first + RIM] + parts[first + RIM : first + 2 * RIM] + parts[first + 2 * RIM : first + 3 * RIM]
        gathered = gathered + (pltpu.roll(part, block * PER_BLOCK, 1) if block else part)
    place = lax.rem(shift + step * blocks * PER_BLOCK, LANES)
    se_out[...] += pltpu.roll(gathered, place, 1)


def middle(piece, bounds, counts, destinations, loaded, arrived, rim, gate, taps, grad, wse, held):
    rows, channels = gate.shape
    part = channels // PIECES
    groups = channels // GROUP
    first = piece * part // BLOCK
    full = lambda height: pl.BlockSpec((height, BLOCK), lambda i: (0, first + i))
    own = lambda height: pl.BlockSpec((height, BLOCK), lambda i: (0, i))
    return pl.pallas_call(
        functools.partial(middle_kernel, (piece * groups // PIECES) % LANES),
        grid=(part // BLOCK,),
        in_specs=[
            SCALARS,
            SCALARS,
            SCALARS,
            pl.BlockSpec((None, None, rows, BLOCK), lambda i: (0, 0, 0, first + i)),
            own(rows + RIM),
            full(RIM),
            full(rows),
            full(taps.shape[0]),
            full(rows),
            full(rows),
        ]
        + [pl.BlockSpec(memory_space=pl.ANY)] * len(held),
        out_specs=[own(rows), full(rows), pl.BlockSpec((RIM, LANES), lambda i: (0, 0))],
        out_shape=[
            jax.ShapeDtypeStruct((rows, part), BF16),
            jax.ShapeDtypeStruct((rows, channels), BF16),
            jax.ShapeDtypeStruct((RIM, LANES), F32),
        ],
        scratch_shapes=[
            pltpu.VMEM((BLOCK // LANES, rows + RIM, LANES), F32),
            pltpu.VMEM((rows, LANES), jnp.int32),
            pltpu.VMEM((LANES, LANES), BF16),
        ],
        input_output_aliases={10: 1} if held else {},
        compiler_params=ROOM,
        cost_estimate=FREE,
    )(bounds, counts, destinations, loaded, arrived, rim, gate, taps, grad, wse, *held)


def lag_kernel(bounds, mid, weighted, after, *rest):
    out, lag_own, lag_next, flip, flipped = rest[-5:]
    rows = mid.shape[0]
    _, bound, later = bounds_near(bounds, rows)

    @pl.when(pl.program_id(0) == 0)
    def _():
        target = grid_of(rows, 1)
        mirrored = rows - 1 - grid_of(rows, 0)
        lag_own[...] = as_mask(same_tile(target, mirrored, bound), F32)
        lag_next[...] = as_mask(tile_before(target, mirrored, later, bound, rows), F32)
        flip[...] = as_mask(mirrored == target, BF16)

    one_row = lax.broadcasted_iota(jnp.int32, (1, LANES), 1) // GROUP
    for block in range(mid.shape[1] // LANES):
        flipped[block] = jnp.dot(flip[...], mid[:, lanes(block * LANES)], preferred_element_type=F32).astype(BF16)
    for block in range(mid.shape[1] // LANES):
        at = lanes(block * LANES)
        pair = jnp.concatenate([weighted[:, at], after[:, at]], axis=0).T
        mirrored_mid = flipped[block]
        lags = []
        for group in range(PER_BLOCK):
            chosen = mirrored_mid * as_mask(one_row == group, BF16)
            products = jnp.dot(chosen, pair, preferred_element_type=F32)
            kept = products[:, :rows] * lag_own[...] + products[:, rows:] * lag_next[...]
            kept = pltpu.roll(kept, 1, 1, stride=1, stride_axis=0)
            lags.append(jnp.sum(kept, axis=0, keepdims=True))
        out[block * PER_BLOCK : (block + 1) * PER_BLOCK] = jnp.concatenate(lags, axis=0)


def lag_grads(piece, bounds, mid, weighted, after, held):
    rows, channels = weighted.shape
    part = channels // PIECES
    first = piece * part // BLOCK
    full = lambda height: pl.BlockSpec((height, BLOCK), lambda i: (0, first + i))
    square = lambda dtype: pltpu.VMEM((rows, rows), dtype)
    return pl.pallas_call(
        lag_kernel,
        grid=(part // BLOCK,),
        in_specs=[SCALARS, pl.BlockSpec((rows, BLOCK), lambda i: (0, i)), full(rows), full(rows)]
        + [pl.BlockSpec(memory_space=pl.ANY)] * len(held),
        out_specs=pl.BlockSpec((BLOCK // GROUP, rows), lambda i: (first + i, 0)),
        out_shape=jax.ShapeDtypeStruct((channels // GROUP, rows), F32),
        scratch_shapes=[square(F32), square(F32), square(BF16), pltpu.VMEM((BLOCK // LANES, rows, LANES), BF16)],
        input_output_aliases={4: 0} if held else {},
        compiler_params=ROOM,
        cost_estimate=FREE,
    )(bounds, mid, weighted, after, *held)


def input_kernel(bounds, grad, wse, taps, out, ext, room):
    rows = out.shape[0]
    earlier, bound, _ = bounds_near(bounds, rows)

    @pl.when(pl.program_id(0) == 0)
    def _():
        row = lax.broadcasted_iota(jnp.int32, (rows, LANES), 0)
        room[:rows] = room_of(row, bound, earlier, rows)
        room[rows:] = jnp.zeros((RIM, LANES), jnp.int32)

    for block in range(out.shape[1] // LANES):
        at = lanes(block * LANES)
        ext[block, :rows] = wse[:, at].astype(F32)
        ext[block, rows:] = jnp.zeros((RIM, LANES), F32)
        total = grad[:, at].astype(F32)
        for lag in range(taps.shape[0] - 1):
            shifted = ext[block, lag : lag + rows]
            total = total + jnp.where(room[lag : lag + rows] >= lag, taps[lag : lag + 1, at] * shifted, 0.0)
        out[:, at] = total.astype(BF16)


def input_grad(bounds, grad, wse, taps):
    rows, channels = grad.shape
    wide = lambda height: pl.BlockSpec((height, BLOCK), lambda i: (0, i))
    return pl.pallas_call(
        input_kernel,
        grid=(channels // BLOCK,),
        in_specs=[SCALARS, wide(rows), wide(rows), wide(taps.shape[0])],
        out_specs=wide(rows),
        out_shape=jax.ShapeDtypeStruct((rows, channels), BF16),
        scratch_shapes=[
            pltpu.VMEM((BLOCK // LANES, rows + RIM, LANES), F32),
            pltpu.VMEM((rows + RIM, LANES), jnp.int32),
        ],
        compiler_params=ROOM,
        cost_estimate=FREE,
    )(bounds, grad, wse, taps)


def rim_kernel(rows, bounds, grad, wse, rim, taps, held, out, ext):
    del held
    some = out.shape[0]
    earlier, bound, later = bounds_near(bounds, rows)
    row = lax.broadcasted_iota(jnp.int32, (some, out.shape[1]), 0) + (rows - some)
    rim_row = lax.broadcasted_iota(jnp.int32, (RIM, out.shape[1]), 0)
    ext[0, :some] = wse[...].astype(F32)
    ext[0, some:] = rim[...].astype(F32)
    ext[1, :some] = room_of(row, bound, earlier, rows).astype(F32)
    ext[1, some:] = room_of(rim_row, later, bound, rows).astype(F32)
    total = grad[...].astype(F32)
    for lag in range(taps.shape[0] - 1):
        shifted = ext[0, lag : lag + some]
        total = total + jnp.where(ext[1, lag : lag + some] >= lag, taps[lag : lag + 1] * shifted, 0.0)
    out[...] = total.astype(BF16)


def rim_grad(bounds, grad, wse, rim, taps, held):
    rows, channels = grad.shape
    some, width = 2 * RIM, channels // 2
    last = pl.BlockSpec((some, width), lambda i: (rows // some - 1, i))
    wide = lambda height: pl.BlockSpec((height, width), lambda i: (0, i))
    return pl.pallas_call(
        functools.partial(rim_kernel, rows),
        grid=(channels // width,),
        in_specs=[SCALARS, last, last, wide(RIM), wide(taps.shape[0]), pl.BlockSpec(memory_space=pl.ANY)],
        out_specs=last,
        out_shape=jax.ShapeDtypeStruct((rows, channels), BF16),
        scratch_shapes=[pltpu.VMEM((2, some + RIM, width), F32)],
        input_output_aliases={5: 0},
        compiler_params=ROOM,
        cost_estimate=FREE,
    )(bounds, grad, wse, rim, taps, held)


def gate_kernel(bounds, prior, mid, incoming, mirrored, *rest):
    out, mask_own, mask_prior = rest[-3:]
    rows = prior.shape[0]
    earlier, bound, _ = bounds_near(bounds, rows)

    @pl.when(pl.program_id(0) == 0)
    def _():
        mask_own[...] = as_mask(same_tile(grid_of(rows, 0), grid_of(rows, 1), bound), BF16)
        mask_prior[...] = as_mask(tile_before(grid_of(rows, 0), grid_of(rows, 1), bound, earlier, rows), BF16)

    for block in range(prior.shape[1] // LANES):
        at = lanes(block * LANES)

        def matrix_of(group):
            line = block * PER_BLOCK + group
            circle = rolled(mirrored[line : line + 1], rows).astype(BF16)
            return jnp.concatenate([circle * mask_own[...], circle * mask_prior[...]], axis=1)

        pair = jnp.concatenate([mid[:, at], prior[:, at]], axis=0)
        out[:, at] = (incoming[:, at].astype(F32) * filtered(matrix_of, pair, rows)).astype(BF16)


def gate_grad(piece, bounds, prior, mid, incoming, mirrored, held):
    rows, channels = incoming.shape
    part = channels // PIECES
    first = piece * part // BLOCK
    full = lambda: pl.BlockSpec((rows, BLOCK), lambda i: (0, first + i))
    own = lambda: pl.BlockSpec((rows, BLOCK), lambda i: (0, i))
    return pl.pallas_call(
        gate_kernel,
        grid=(part // BLOCK,),
        in_specs=[SCALARS, own(), own(), full(), pl.BlockSpec((BLOCK // GROUP, rows), lambda i: (first + i, 0))]
        + [pl.BlockSpec(memory_space=pl.ANY)] * len(held),
        out_specs=full(),
        out_shape=jax.ShapeDtypeStruct((rows, channels), BF16),
        scratch_shapes=[pltpu.VMEM((rows, rows), BF16)] * 2,
        input_output_aliases={5: 0} if held else {},
        compiler_params=ROOM,
        cost_estimate=FREE,
    )(bounds, prior, mid, incoming, mirrored, *held)


def body(loaded, counts, destinations, bounds, se_gate, mr_gate, phase_grads, se_taps, mr_taps):
    ctx_count = lax.axis_size("ctx")
    rows, channels = loaded.shape[2:]
    group_count = channels // GROUP
    gate_se = se_gate[0]

    incoming = partner(phase_grads[0], "pipe", 1)
    weighted = (mr_gate[0].astype(F32) * incoming.astype(F32)).astype(BF16)
    after = from_behind(weighted, "ctx", -1)
    low, mirrored, taps_se = taps_forms(mr_taps[0], se_taps[0])
    base = own_back(bounds, weighted, incoming, low)

    *outgoing, sent_tail = pick_outgoing(counts, destinations, loaded)
    shards = range(ctx_count - 2)
    rim = lax.ppermute(sent_tail, "ctx", [(i, i + 2) for i in shards if i % 4 != 1])
    rim_last = lax.ppermute(sent_tail, "ctx", [(i, i + 2) for i in shards if i % 4 == 1])
    after, rim, base, low, mirrored, taps_se, *outgoing = lax.optimization_barrier(
        (after, rim, base, low, mirrored, taps_se, *outgoing)
    )
    arrived = [from_behind(piece, "ctx", 1) for piece in outgoing]

    mid_grad, wse = next_back(bounds, after, base, gate_se, low)
    mid_grad, rim, rim_last = lax.optimization_barrier((mid_grad, rim, rim_last))
    rim = rim + rim_last
    grad_x = input_grad(bounds, mid_grad, wse, taps_se)
    arrived[0], grad_x = lax.optimization_barrier((arrived[0], grad_x))

    mid, prior, se_sums, gates, lags = [], [], [], (), ()
    for q in range(PIECES):
        mid_piece, gate_piece, se_sum = middle(
            q, bounds, counts, destinations, loaded, arrived[q], rim, gate_se, taps_se, mid_grad, wse, gates
        )
        gates = (gate_piece,)
        lags = (lag_grads(q, bounds, mid_piece, weighted, after, lags),)
        mid.append(mid_piece)
        se_sums.append(se_sum)
        if q < PIECES - 1:
            prior.append(from_behind(mid_piece, "ctx", 1))
    grad_gate_se = gates[0]

    windows = max(group_count // LANES, 1)
    each = PIECES // windows
    se_windows = [sum(se_sums[w * each : (w + 1) * each]) for w in range(windows)]
    total = jnp.concatenate([lags[0], *se_windows], axis=0)
    total, mid[-1] = lax.optimization_barrier((total, mid[-1]))
    prior.append(from_behind(mid[-1], "ctx", 1))
    grad_gate_mr = (gate_grad(0, bounds, prior[0], mid[0], incoming, mirrored, ()),)
    total, wse, *grad_gate_mr = lax.optimization_barrier((total, wse, *grad_gate_mr))
    rim_next = from_behind(wse[:RIM], "ctx", -1)

    mask = ctx_count // 2
    while mask > 2:
        total = total + partner(total, "ctx", mask)
        if mask == 4:
            for q in range(1, PIECES):
                grad_gate_mr = (gate_grad(q, bounds, prior[q], mid[q], incoming, mirrored, tuple(grad_gate_mr)),)
            total, *grad_gate_mr = lax.optimization_barrier((total, *grad_gate_mr))
        else:
            total, rim_next = lax.optimization_barrier((total, rim_next))
        mask //= 2
    one, two, three = (partner(total, "ctx", mask) for mask in (1, 2, 3))
    grad_x = rim_grad(bounds, mid_grad, wse, rim_next, taps_se, grad_x)
    total = (total + one) + (two + three)

    scale = 1.0 / math.sqrt(ctx_count * rows * GROUP)
    total = total * scale
    mr_total = total[:group_count]
    se_total = total[group_count:].reshape(windows, RIM, -1).transpose(0, 2, 1)
    se_total = se_total.reshape(group_count, RIM)[:, : se_taps.shape[2]]
    return (grad_x[None], grad_gate_se[None], grad_gate_mr[0][None], se_total[None], mr_total[None])


def solution(mesh):
    return jax.shard_map(
        body,
        mesh=mesh,
        in_specs=(
            P("pipe", "ctx", None, None),
            P("ctx"),
            P("ctx"),
            P(),
            P("pipe", "ctx", None),
            P("pipe", "ctx", None),
            P("pipe", "ctx", None),
            P("pipe", None, None),
            P("pipe", None, None),
        ),
        out_specs=(
            P("pipe", "ctx", None),
            P("pipe", "ctx", None),
            P("pipe", "ctx", None),
            P("pipe", None, None),
            P("pipe", None, None),
        ),
        check_vma=False,
    )
```

```python
import functools
import math

import jax
import jax.numpy as jnp
from jax import lax
from jax.experimental import pallas as pl
from jax.experimental.pallas import tpu as pltpu
from jax.sharding import PartitionSpec as P

GROUP = 16
LANES = 128
PER_BLOCK = LANES // GROUP
RIM = 8
FAR = 1 << 20
PIECES = 2
BLOCK = 2048

F32 = jnp.float32
BF16 = jnp.bfloat16


def from_behind(block, axis, distance):
    devices = range(lax.axis_size(axis))
    route = [(i - distance, i) for i in devices if i - distance in devices]
    return lax.ppermute(block, axis, route)


def partner(value, axis, mask):
    pairs = [(source, source ^ mask) for source in range(lax.axis_size(axis))]
    return lax.ppermute(value, axis, pairs)


def exchange_order(count):
    masks = [1 << bit for bit in range(count.bit_length() - 1)]
    return masks[1:] + masks[:1]


def grid_of(rows, which):
    return lax.broadcasted_iota(jnp.int32, (rows, rows), which)


def same_tile(out_row, in_row, bound):
    return (out_row >= in_row) & ((out_row < bound) | (in_row >= bound))


def tile_before(out_row, in_row, bound, earlier, rows):
    return (out_row < in_row) & (out_row < bound) & ((earlier >= rows) | (in_row >= earlier))


def as_mask(flags, dtype):
    return jnp.where(flags, 1.0, 0.0).astype(F32).astype(dtype)


def room_of(row, bound, earlier, rows):
    before = jnp.where(earlier < rows, row + (rows - earlier), FAR)
    return jnp.where(row >= bound, row - bound, before)


def rolled(line, rows):
    return pltpu.roll(jnp.broadcast_to(line, (rows, rows)), 0, 1, stride=1, stride_axis=0)


def lanes(start):
    return pl.ds(start, LANES)


def bounds_near(bounds, rows):
    count = bounds.shape[0]
    shard = lax.axis_index("ctx")
    near = []
    for tile in (shard - 1, shard, shard + 1):
        bound = bounds[jnp.clip(tile, 0, count - 1)]
        near.append(jnp.where((tile >= 0) & (tile < count), bound, rows))
    return near


def holds_own(counts, destinations):
    return (counts[0] >= 1) & (destinations[0] == lax.axis_index("ctx"))


SCALARS = pl.BlockSpec(memory_space=pltpu.SMEM)
FREE = pl.CostEstimate(flops=1, bytes_accessed=1, transcendentals=0)
ROOM = pltpu.CompilerParams(vmem_limit_bytes=40 << 20)


def pick_kernel(counts, destinations, slot, first, *outs):
    *pieces, sent_tail = outs
    rows = slot.shape[0]
    shard = lax.axis_index("ctx")
    sends = ((counts[0] >= 1) & (destinations[0] == shard + 1)) | ((counts[0] >= 2) & (destinations[1] == shard + 1))
    picked = slot[...]
    own = jnp.where(holds_own(counts, destinations), first[...].astype(F32), 0.0)[-RIM:].astype(BF16)
    for number, piece in enumerate(pieces):

        @pl.when(pl.program_id(0) == number)
        def _(piece=piece):
            piece[:rows] = picked
            piece[rows:] = own

    sent_tail[...] = jnp.where(sends, picked[-2 * RIM :].astype(F32), 0.0)[-RIM:].astype(BF16)


def pick_outgoing(counts, destinations, loaded):
    rows, channels = loaded.shape[2:]
    width = channels // PIECES
    shape = lambda height, size: jax.ShapeDtypeStruct((height, size), loaded.dtype)
    return pl.pallas_call(
        pick_kernel,
        grid_spec=pltpu.PrefetchScalarGridSpec(
            num_scalar_prefetch=2,
            grid=(PIECES,),
            in_specs=[
                pl.BlockSpec((None, None, rows, width), lambda i, held, _: (0, jnp.where(held[0] == 2, 1, 0), 0, i)),
                pl.BlockSpec((None, None, 2 * RIM, width), lambda i, *_: (0, 0, rows // (2 * RIM) - 1, i)),
            ],
            out_specs=[pl.BlockSpec((rows + RIM, width), lambda i, *_: (0, 0))] * PIECES
            + [pl.BlockSpec((RIM, width), lambda i, *_: (0, i))],
        ),
        out_shape=[shape(rows + RIM, width)] * PIECES + [shape(RIM, channels)],
        cost_estimate=FREE,
    )(counts, destinations, loaded, loaded)


def taps_kernel(mr, se, low, mirrored, spread):
    groups, count = mr.shape
    rounded = mr[...].astype(BF16)
    low[...] = rounded.astype(F32)
    mirror = as_mask(lax.rem(grid_of(count, 0) + grid_of(count, 1), count) == 0, BF16)
    mirrored[...] = jnp.dot(rounded, mirror, preferred_element_type=F32)
    taps = se.shape[1]
    group = lax.broadcasted_iota(jnp.int32, (PER_BLOCK, LANES), 0)
    owner = lax.broadcasted_iota(jnp.int32, (PER_BLOCK, LANES), 1) // GROUP
    widen = as_mask(group == owner, F32)
    for block in range(groups // PER_BLOCK):
        part = se[block * PER_BLOCK : (block + 1) * PER_BLOCK]
        for tap in range(taps):
            line = jnp.sum(part[:, tap : tap + 1] * widen, axis=0, keepdims=True)
            spread[tap : tap + 1, lanes(block * LANES)] = line
    spread[taps:] = jnp.zeros((spread.shape[0] - taps, spread.shape[1]), F32)


def taps_forms(mr_taps, se_taps):
    groups, count = mr_taps.shape
    return pl.pallas_call(
        taps_kernel,
        out_shape=[
            jax.ShapeDtypeStruct((groups, count), F32),
            jax.ShapeDtypeStruct((groups, count), F32),
            jax.ShapeDtypeStruct((RIM, groups * GROUP), F32),
        ],
        cost_estimate=FREE,
    )(mr_taps, se_taps)


def filtered(matrix_of, values, rows):
    lane_group = lax.broadcasted_iota(jnp.int32, (rows, LANES), 1) // GROUP
    total = jnp.zeros((rows, LANES), F32)
    for group in range(PER_BLOCK):
        product = jnp.dot(matrix_of(group), values, preferred_element_type=F32)
        total = jnp.where(lane_group == group, product, total)
    return total


def own_back_kernel(bounds, weighted, incoming, low, out, mask):
    rows = weighted.shape[0]
    _, bound, _ = bounds_near(bounds, rows)

    @pl.when(pl.program_id(0) == 0)
    def _():
        mask[...] = as_mask(same_tile(grid_of(rows, 1), grid_of(rows, 0), bound), BF16)

    for block in range(weighted.shape[1] // LANES):
        at = lanes(block * LANES)

        def matrix_of(group):
            line = block * PER_BLOCK + group
            return rolled(low[line : line + 1], rows).astype(BF16) * mask[...]

        out[:, at] = incoming[:, at].astype(F32) + filtered(matrix_of, weighted[:, at], rows)


def own_back(bounds, weighted, incoming, low):
    rows, channels = weighted.shape
    wide = lambda height: pl.BlockSpec((height, BLOCK), lambda i: (0, i))
    return pl.pallas_call(
        own_back_kernel,
        grid=(channels // BLOCK,),
        in_specs=[SCALARS, wide(rows), wide(rows), pl.BlockSpec((BLOCK // GROUP, rows), lambda i: (i, 0))],
        out_specs=wide(rows),
        out_shape=jax.ShapeDtypeStruct((rows, channels), F32),
        scratch_shapes=[pltpu.VMEM((rows, rows), BF16)],
        compiler_params=ROOM,
        cost_estimate=FREE,
    )(bounds, weighted, incoming, low)


def next_back_kernel(bounds, after, base, gate, low, mid_grad, wse, mask):
    rows = after.shape[0]
    _, bound, later = bounds_near(bounds, rows)

    @pl.when(pl.program_id(0) == 0)
    def _():
        mask[...] = as_mask(tile_before(grid_of(rows, 1), grid_of(rows, 0), later, bound, rows), BF16)

    for block in range(after.shape[1] // LANES):
        at = lanes(block * LANES)

        def matrix_of(group):
            line = block * PER_BLOCK + group
            return rolled(low[line : line + 1], rows).astype(BF16) * mask[...]

        grad = (base[:, at] + filtered(matrix_of, after[:, at], rows)).astype(BF16)
        mid_grad[:, at] = grad
        wse[:, at] = (gate[:, at].astype(F32) * grad.astype(F32)).astype(BF16)


def next_back(bounds, after, base, gate, low):
    rows, channels = after.shape
    wide = lambda height: pl.BlockSpec((height, BLOCK), lambda i: (0, i))
    return pl.pallas_call(
        next_back_kernel,
        grid=(channels // BLOCK,),
        in_specs=[
            SCALARS,
            wide(rows),
            wide(rows),
            wide(rows),
            pl.BlockSpec((BLOCK // GROUP, rows), lambda i: (i, 0)),
        ],
        out_specs=[wide(rows)] * 2,
        out_shape=[jax.ShapeDtypeStruct((rows, channels), BF16)] * 2,
        scratch_shapes=[pltpu.VMEM((rows, rows), BF16)],
        compiler_params=ROOM,
        cost_estimate=FREE,
    )(bounds, after, base, gate, low)


def middle_kernel(shift, bounds, counts, destinations, slot, arrived, rim, gate, taps, grad, wse, *rest):
    mid_out, gate_grad, se_out, ext, room, spread = rest[-6:]
    rows = slot.shape[0]
    step = pl.program_id(0)
    earlier, bound, _ = bounds_near(bounds, rows)
    own_here = holds_own(counts, destinations)

    @pl.when(step == 0)
    def _():
        row = lax.broadcasted_iota(jnp.int32, (rows, LANES), 0)
        room[...] = room_of(row, bound, earlier, rows)
        se_out[...] = jnp.zeros_like(se_out)
        spread[...] = as_mask(grid_of(LANES, 0) // GROUP == grid_of(LANES, 1), BF16)

    blocks = slot.shape[1] // LANES
    thirds = []
    for block in range(blocks):
        at = lanes(block * LANES)
        x = jnp.where(own_here, slot[:, at].astype(F32), arrived[:rows, at].astype(F32))
        ext[block, :RIM] = arrived[rows:, at].astype(F32) + rim[:, at].astype(F32)
        ext[block, RIM:] = x
        mix = jnp.zeros((rows, LANES), F32)
        wide_wse = wse[:, at].astype(F32)
        sums = []
        for lag in range(taps.shape[0] - 1):
            kept = jnp.where(room[...] >= lag, ext[block, RIM - lag : RIM - lag + rows], 0.0)
            mix = mix + taps[lag : lag + 1, at] * kept
            sums.append(jnp.sum(wide_wse * kept, axis=0, keepdims=True))
        sums.append(jnp.zeros((1, LANES), F32))
        mid_out[:, at] = (x + gate[:, at].astype(F32) * mix).astype(BF16)
        gate_grad[:, at] = (grad[:, at].astype(F32) * mix).astype(BF16)
        left = jnp.concatenate(sums, axis=0)
        for _ in range(3):
            term = left.astype(BF16).astype(F32)
            thirds.append(term)
            left = left - term
    parts = jnp.dot(jnp.concatenate(thirds, axis=0).astype(BF16), spread[...], preferred_element_type=F32)
    gathered = jnp.zeros((RIM, LANES), F32)
    for block in range(blocks):
        first = 3 * RIM * block
        part = parts[first : first + RIM] + parts[first + RIM : first + 2 * RIM] + parts[first + 2 * RIM : first + 3 * RIM]
        gathered = gathered + (pltpu.roll(part, block * PER_BLOCK, 1) if block else part)
    place = lax.rem(shift + step * blocks * PER_BLOCK, LANES)
    se_out[...] += pltpu.roll(gathered, place, 1)


def middle(piece, bounds, counts, destinations, loaded, arrived, rim, gate, taps, grad, wse, held):
    rows, channels = gate.shape
    part = channels // PIECES
    groups = channels // GROUP
    first = piece * part // BLOCK
    full = lambda height: pl.BlockSpec((height, BLOCK), lambda i: (0, first + i))
    own = lambda height: pl.BlockSpec((height, BLOCK), lambda i: (0, i))
    return pl.pallas_call(
        functools.partial(middle_kernel, (piece * groups // PIECES) % LANES),
        grid=(part // BLOCK,),
        in_specs=[
            SCALARS,
            SCALARS,
            SCALARS,
            pl.BlockSpec((None, None, rows, BLOCK), lambda i: (0, 0, 0, first + i)),
            own(rows + RIM),
            full(RIM),
            full(rows),
            full(taps.shape[0]),
            full(rows),
            full(rows),
        ]
        + [pl.BlockSpec(memory_space=pl.ANY)] * len(held),
        out_specs=[own(rows), full(rows), pl.BlockSpec((RIM, LANES), lambda i: (0, 0))],
        out_shape=[
            jax.ShapeDtypeStruct((rows, part), BF16),
            jax.ShapeDtypeStruct((rows, channels), BF16),
            jax.ShapeDtypeStruct((RIM, LANES), F32),
        ],
        scratch_shapes=[
            pltpu.VMEM((BLOCK // LANES, rows + RIM, LANES), F32),
            pltpu.VMEM((rows, LANES), jnp.int32),
            pltpu.VMEM((LANES, LANES), BF16),
        ],
        input_output_aliases={10: 1} if held else {},
        compiler_params=ROOM,
        cost_estimate=FREE,
    )(bounds, counts, destinations, loaded, arrived, rim, gate, taps, grad, wse, *held)


def lag_kernel(bounds, mid, weighted, after, *rest):
    out, lag_own, lag_next, flip, flipped = rest[-5:]
    rows = mid.shape[0]
    _, bound, later = bounds_near(bounds, rows)

    @pl.when(pl.program_id(0) == 0)
    def _():
        target = grid_of(rows, 1)
        mirrored = rows - 1 - grid_of(rows, 0)
        lag_own[...] = as_mask(same_tile(target, mirrored, bound), F32)
        lag_next[...] = as_mask(tile_before(target, mirrored, later, bound, rows), F32)
        flip[...] = as_mask(mirrored == target, BF16)

    one_row = lax.broadcasted_iota(jnp.int32, (1, LANES), 1) // GROUP
    for block in range(mid.shape[1] // LANES):
        flipped[block] = jnp.dot(flip[...], mid[:, lanes(block * LANES)], preferred_element_type=F32).astype(BF16)
    for block in range(mid.shape[1] // LANES):
        at = lanes(block * LANES)
        pair = jnp.concatenate([weighted[:, at], after[:, at]], axis=0).T
        mirrored_mid = flipped[block]
        lags = []
        for group in range(PER_BLOCK):
            chosen = mirrored_mid * as_mask(one_row == group, BF16)
            products = jnp.dot(chosen, pair, preferred_element_type=F32)
            kept = products[:, :rows] * lag_own[...] + products[:, rows:] * lag_next[...]
            kept = pltpu.roll(kept, 1, 1, stride=1, stride_axis=0)
            lags.append(jnp.sum(kept, axis=0, keepdims=True))
        out[block * PER_BLOCK : (block + 1) * PER_BLOCK] = jnp.concatenate(lags, axis=0)


def lag_grads(piece, bounds, mid, weighted, after, held):
    rows, channels = weighted.shape
    part = channels // PIECES
    first = piece * part // BLOCK
    full = lambda height: pl.BlockSpec((height, BLOCK), lambda i: (0, first + i))
    square = lambda dtype: pltpu.VMEM((rows, rows), dtype)
    return pl.pallas_call(
        lag_kernel,
        grid=(part // BLOCK,),
        in_specs=[SCALARS, pl.BlockSpec((rows, BLOCK), lambda i: (0, i)), full(rows), full(rows)]
        + [pl.BlockSpec(memory_space=pl.ANY)] * len(held),
        out_specs=pl.BlockSpec((BLOCK // GROUP, rows), lambda i: (first + i, 0)),
        out_shape=jax.ShapeDtypeStruct((channels // GROUP, rows), F32),
        scratch_shapes=[square(F32), square(F32), square(BF16), pltpu.VMEM((BLOCK // LANES, rows, LANES), BF16)],
        input_output_aliases={4: 0} if held else {},
        compiler_params=ROOM,
        cost_estimate=FREE,
    )(bounds, mid, weighted, after, *held)


def input_kernel(bounds, grad, wse, taps, out, ext, room):
    rows = out.shape[0]
    earlier, bound, _ = bounds_near(bounds, rows)

    @pl.when(pl.program_id(0) == 0)
    def _():
        row = lax.broadcasted_iota(jnp.int32, (rows, LANES), 0)
        room[:rows] = room_of(row, bound, earlier, rows)
        room[rows:] = jnp.zeros((RIM, LANES), jnp.int32)

    for block in range(out.shape[1] // LANES):
        at = lanes(block * LANES)
        ext[block, :rows] = wse[:, at].astype(F32)
        ext[block, rows:] = jnp.zeros((RIM, LANES), F32)
        total = grad[:, at].astype(F32)
        for lag in range(taps.shape[0] - 1):
            shifted = ext[block, lag : lag + rows]
            total = total + jnp.where(room[lag : lag + rows] >= lag, taps[lag : lag + 1, at] * shifted, 0.0)
        out[:, at] = total.astype(BF16)


def input_grad(bounds, grad, wse, taps):
    rows, channels = grad.shape
    wide = lambda height: pl.BlockSpec((height, BLOCK), lambda i: (0, i))
    return pl.pallas_call(
        input_kernel,
        grid=(channels // BLOCK,),
        in_specs=[SCALARS, wide(rows), wide(rows), wide(taps.shape[0])],
        out_specs=wide(rows),
        out_shape=jax.ShapeDtypeStruct((rows, channels), BF16),
        scratch_shapes=[
            pltpu.VMEM((BLOCK // LANES, rows + RIM, LANES), F32),
            pltpu.VMEM((rows + RIM, LANES), jnp.int32),
        ],
        compiler_params=ROOM,
        cost_estimate=FREE,
    )(bounds, grad, wse, taps)


def rim_kernel(rows, bounds, grad, wse, rim, taps, held, out, ext):
    del held
    some = out.shape[0]
    earlier, bound, later = bounds_near(bounds, rows)
    row = lax.broadcasted_iota(jnp.int32, (some, out.shape[1]), 0) + (rows - some)
    rim_row = lax.broadcasted_iota(jnp.int32, (RIM, out.shape[1]), 0)
    ext[0, :some] = wse[...].astype(F32)
    ext[0, some:] = rim[...].astype(F32)
    ext[1, :some] = room_of(row, bound, earlier, rows).astype(F32)
    ext[1, some:] = room_of(rim_row, later, bound, rows).astype(F32)
    total = grad[...].astype(F32)
    for lag in range(taps.shape[0] - 1):
        shifted = ext[0, lag : lag + some]
        total = total + jnp.where(ext[1, lag : lag + some] >= lag, taps[lag : lag + 1] * shifted, 0.0)
    out[...] = total.astype(BF16)


def rim_grad(bounds, grad, wse, rim, taps, held):
    rows, channels = grad.shape
    some, width = 2 * RIM, channels // 2
    last = pl.BlockSpec((some, width), lambda i: (rows // some - 1, i))
    wide = lambda height: pl.BlockSpec((height, width), lambda i: (0, i))
    return pl.pallas_call(
        functools.partial(rim_kernel, rows),
        grid=(channels // width,),
        in_specs=[SCALARS, last, last, wide(RIM), wide(taps.shape[0]), pl.BlockSpec(memory_space=pl.ANY)],
        out_specs=last,
        out_shape=jax.ShapeDtypeStruct((rows, channels), BF16),
        scratch_shapes=[pltpu.VMEM((2, some + RIM, width), F32)],
        input_output_aliases={5: 0},
        compiler_params=ROOM,
        cost_estimate=FREE,
    )(bounds, grad, wse, rim, taps, held)


def gate_kernel(bounds, prior, mid, incoming, mirrored, *rest):
    out, mask_own, mask_prior = rest[-3:]
    rows = prior.shape[0]
    earlier, bound, _ = bounds_near(bounds, rows)

    @pl.when(pl.program_id(0) == 0)
    def _():
        mask_own[...] = as_mask(same_tile(grid_of(rows, 0), grid_of(rows, 1), bound), BF16)
        mask_prior[...] = as_mask(tile_before(grid_of(rows, 0), grid_of(rows, 1), bound, earlier, rows), BF16)

    for block in range(prior.shape[1] // LANES):
        at = lanes(block * LANES)

        def matrix_of(group):
            line = block * PER_BLOCK + group
            circle = rolled(mirrored[line : line + 1], rows).astype(BF16)
            return jnp.concatenate([circle * mask_own[...], circle * mask_prior[...]], axis=1)

        pair = jnp.concatenate([mid[:, at], prior[:, at]], axis=0)
        out[:, at] = (incoming[:, at].astype(F32) * filtered(matrix_of, pair, rows)).astype(BF16)


def gate_grad(piece, bounds, prior, mid, incoming, mirrored, held):
    rows, channels = incoming.shape
    part = channels // PIECES
    first = piece * part // BLOCK
    full = lambda: pl.BlockSpec((rows, BLOCK), lambda i: (0, first + i))
    own = lambda: pl.BlockSpec((rows, BLOCK), lambda i: (0, i))
    return pl.pallas_call(
        gate_kernel,
        grid=(part // BLOCK,),
        in_specs=[SCALARS, own(), own(), full(), pl.BlockSpec((BLOCK // GROUP, rows), lambda i: (first + i, 0))]
        + [pl.BlockSpec(memory_space=pl.ANY)] * len(held),
        out_specs=full(),
        out_shape=jax.ShapeDtypeStruct((rows, channels), BF16),
        scratch_shapes=[pltpu.VMEM((rows, rows), BF16)] * 2,
        input_output_aliases={5: 0} if held else {},
        compiler_params=ROOM,
        cost_estimate=FREE,
    )(bounds, prior, mid, incoming, mirrored, *held)


def body(loaded, counts, destinations, bounds, se_gate, mr_gate, phase_grads, se_taps, mr_taps):
    ctx_count = lax.axis_size("ctx")
    rows, channels = loaded.shape[2:]
    group_count = channels // GROUP
    gate_se = se_gate[0]

    incoming = partner(phase_grads[0], "pipe", 1)
    weighted = (mr_gate[0].astype(F32) * incoming.astype(F32)).astype(BF16)
    after = from_behind(weighted, "ctx", -1)
    low, mirrored, taps_se = taps_forms(mr_taps[0], se_taps[0])
    base = own_back(bounds, weighted, incoming, low)

    *outgoing, sent_tail = pick_outgoing(counts, destinations, loaded)
    shards = range(ctx_count - 2)
    rim = lax.ppermute(sent_tail, "ctx", [(i, i + 2) for i in shards if i % 4 != 1])
    rim_last = lax.ppermute(sent_tail, "ctx", [(i, i + 2) for i in shards if i % 4 == 1])
    after, rim, base, low, mirrored, taps_se, *outgoing = lax.optimization_barrier(
        (after, rim, base, low, mirrored, taps_se, *outgoing)
    )
    arrived = [from_behind(piece, "ctx", 1) for piece in outgoing]

    mid_grad, wse = next_back(bounds, after, base, gate_se, low)
    mid_grad, rim, rim_last = lax.optimization_barrier((mid_grad, rim, rim_last))
    rim = rim + rim_last
    grad_x = input_grad(bounds, mid_grad, wse, taps_se)
    arrived[0], grad_x = lax.optimization_barrier((arrived[0], grad_x))

    mid, prior, se_sums, gates, lags = [], [], [], (), ()
    for q in range(PIECES):
        mid_piece, gate_piece, se_sum = middle(
            q, bounds, counts, destinations, loaded, arrived[q], rim, gate_se, taps_se, mid_grad, wse, gates
        )
        gates = (gate_piece,)
        lags = (lag_grads(q, bounds, mid_piece, weighted, after, lags),)
        mid.append(mid_piece)
        se_sums.append(se_sum)
        if q < PIECES - 1:
            prior.append(from_behind(mid_piece, "ctx", 1))
    grad_gate_se = gates[0]

    windows = max(group_count // LANES, 1)
    each = PIECES // windows
    se_windows = [sum(se_sums[w * each : (w + 1) * each]) for w in range(windows)]
    total = jnp.concatenate([lags[0], *se_windows], axis=0)
    total, mid[-1] = lax.optimization_barrier((total, mid[-1]))
    prior.append(from_behind(mid[-1], "ctx", 1))
    grad_gate_mr = (gate_grad(0, bounds, prior[0], mid[0], incoming, mirrored, ()),)
    total, wse, *grad_gate_mr = lax.optimization_barrier((total, wse, *grad_gate_mr))
    rim_next = from_behind(wse[:RIM], "ctx", -1)

    mask = ctx_count // 2
    while mask > 2:
        total = total + partner(total, "ctx", mask)
        if mask == 4:
            grad_x = rim_grad(bounds, mid_grad, wse, rim_next, taps_se, grad_x)
            total, grad_x, *prior[1:] = lax.optimization_barrier((total, grad_x, *prior[1:]))
        else:
            total, rim_next = lax.optimization_barrier((total, rim_next))
        mask //= 2
    one, two, three = (partner(total, "ctx", mask) for mask in (1, 2, 3))
    for q in range(1, PIECES):
        grad_gate_mr = (gate_grad(q, bounds, prior[q], mid[q], incoming, mirrored, tuple(grad_gate_mr)),)
    total = (total + one) + (two + three)

    scale = 1.0 / math.sqrt(ctx_count * rows * GROUP)
    total = total * scale
    mr_total = total[:group_count]
    se_total = total[group_count:].reshape(windows, RIM, -1).transpose(0, 2, 1)
    se_total = se_total.reshape(group_count, RIM)[:, : se_taps.shape[2]]
    return (grad_x[None], grad_gate_se[None], grad_gate_mr[0][None], se_total[None], mr_total[None])


def solution(mesh):
    return jax.shard_map(
        body,
        mesh=mesh,
        in_specs=(
            P("pipe", "ctx", None, None),
            P("ctx"),
            P("ctx"),
            P(),
            P("pipe", "ctx", None),
            P("pipe", "ctx", None),
            P("pipe", "ctx", None),
            P("pipe", None, None),
            P("pipe", None, None),
        ),
        out_specs=(
            P("pipe", "ctx", None),
            P("pipe", "ctx", None),
            P("pipe", "ctx", None),
            P("pipe", None, None),
            P("pipe", None, None),
        ),
        check_vma=False,
    )
```
